256 devices in a mesh: cube: 8 (over y, x_lo), grid: 32 (over x_hi, z, core).
Axes of the slice: x: 4 (x_hi: 2, x_lo: 2; x = x_hi * 2 + x_lo), y: 4, z: 8, core: 2. Of those that a mesh axis runs over, the one named last changes fastest.
Arguments:
- panel: float32 [8, 2048, 512], P('cube', 'grid'), may hold values from -0.25 to 0.25
- pattern: int32 [8, 8, 2], P('cube'), may hold values 0 or 1
- child_inverse: float32 [8, 512, 512], P('cube'), as said below
- ext_map: int32 [8, 8], replicated, may hold values from 0 to 17, as said below
- upper_rows: float32 [8, 2048, 512], P('cube', 'grid'), may hold values from -0.625 to 0.625
- parent_inverse: float32 [8, 256, 512], P('cube'), as said below
- update_block: float32 [8, 2048, 4096], P('cube', None, 'grid'), as said below
Outputs:
- schur: float32 [8, 2048, 4096], P('cube', None, 'grid')
The draws below stay inside these ranges and needn't reach their ends.
Inputs may be any that keep to these rules, and one draw needn't show every extreme that they name: `ext_map`: within each row the 8 entries are distinct parent tiles. Each child_inverse[c] is lower triangular with positive diagonal. `parent_inverse`: each parent's two halves together form a lower triangular matrix with positive diagonal. `update_block`: each parent's two halves together form a symmetric matrix.
All inputs are finite; a program needn't handle non-finite values. No bound on the sum of `pattern` on one device may be relied on, other than what follows from the above.
Results may differ from the reference program's by a relative error of at most 0.00011.
Values sent between devices are 32-bit elements; how exact they have to be, the bound alone decides.
A program may use at most 128 MiB of HBM per device.

```python
import math
import jax
import jax.numpy as jnp
from jax import lax

TILE = 256
PC = 512
MC = 2048
PP = 512
MP = 4096
CT = 8
FT = 18
N_CUBE = 8


def lower_factor(key, group_count, order_size, diag_low, diag_high):
    key_lower, key_diagonal = jax.random.split(key)
    lower_part = jax.random.normal(key_lower, (group_count, order_size, order_size), jnp.float32) * (0.5 / math.sqrt(order_size))
    lower_part = jnp.tril(lower_part, -1)
    diagonal = jax.random.uniform(key_diagonal, (group_count, order_size), jnp.float32, diag_low, diag_high)
    return lower_part + diagonal[:, :, None] * jnp.eye(order_size, dtype=jnp.float32)[None]


def draw_child_inverse(key, part):
    key = jax.random.fold_in(key, 1)
    return lower_factor(key, N_CUBE, PC, 0.5, 1.5)


def draw_parent_inverse(key, part):
    key = jax.random.fold_in(key, 2)
    entries = lower_factor(key, N_CUBE // 2, PP, 0.5, 1.5)
    return entries.reshape(N_CUBE, PP // 2, PP)


def draw_ext_map(key, part):
    key = jax.random.fold_in(key, 3)
    row_keys = jax.random.split(key, N_CUBE)
    return jax.vmap(lambda sub_key: jax.random.permutation(sub_key, FT)[:CT])(row_keys).astype(jnp.int32)


def draw_update_block(key, part):
    key = jax.random.fold_in(key, 4)
    entries = jax.random.normal(key, (N_CUBE // 2, MP, MP), jnp.float32)
    symmetric = (entries + jnp.swapaxes(entries, 1, 2)) * (0.1 / math.sqrt(2.0))
    return symmetric.reshape(N_CUBE, MP // 2, MP)


def set_ends(result, stream_key, least, largest):
    longest = result.shape.index(max(result.shape))
    spots = []
    for shift in (0, 1):
        where = [jax.random.randint(jax.random.fold_in(stream_key, axis), (), 0, length) for axis, length in enumerate(result.shape)]
        where[longest] = (where[longest] + shift) % result.shape[longest]
        spots.append(tuple(where))
    return result.at[spots[0]].set(least).at[spots[1]].set(largest)


def steps_of(stream_key, dims, shards, least, largest):
    def one(axis_at, parts):
        steps = jax.random.uniform(jax.random.fold_in(jax.random.fold_in(stream_key, 6), axis_at), (parts,), jnp.float32, least / len(shards), largest / len(shards))
        return jnp.repeat(jnp.exp(steps), dims[axis_at] // parts).reshape((-1,) + (1,) * (len(dims) - axis_at - 1))

    gain = one(*shards[0])
    for cut in shards[1:]:
        gain = gain * one(*cut)
    return gain


def centred(own_key, shape, spread, reach, shards=(), held_as=jnp.bfloat16):
    level = steps_of(own_key, shape, shards, -0.22, 0.18) if shards else 1.0
    values = jax.random.normal(own_key, shape, jnp.float32) * spread * level
    return jnp.minimum(jnp.maximum(values, -reach), reach).astype(held_as)


def setup_inputs(seed: int = 0) -> dict:
    key_list = jax.random.split(jax.random.key(seed), 8)
    panel = centred(key_list[0], (N_CUBE, MC, PC), PC ** -0.5, 0.25, ((0, 8), (1, 32)), jnp.float32)
    pattern = set_ends((jax.random.randint(key_list[1], (N_CUBE, CT, PC // TILE), 0, 3) < 2).astype(jnp.int32), jax.random.fold_in(key_list[1], 1), 0, 1)
    child_inverse = draw_child_inverse(jax.random.fold_in(key_list[7], 71), 0)
    ext_map = draw_ext_map(jax.random.fold_in(key_list[7], 71), 0)
    upper_rows = centred(key_list[4], (N_CUBE, MP // 2, PP), 0.04, 0.625, ((0, 8), (1, 32)), jnp.float32)
    parent_inverse = draw_parent_inverse(jax.random.fold_in(key_list[7], 71), 0)
    update_block = draw_update_block(jax.random.fold_in(key_list[7], 71), 0)
    return dict(panel=panel, pattern=pattern, child_inverse=child_inverse, ext_map=ext_map, upper_rows=upper_rows, parent_inverse=parent_inverse, update_block=update_block)


def product(left, right):
    return jnp.dot(left, right, precision=lax.Precision.HIGHEST, preferred_element_type=jnp.float32)


def child_rows(panel_rows, pattern_rows, inverse, start_row, tile_size):
    row_count = panel_rows.shape[0]
    row_ids = start_row + jnp.arange(row_count, dtype=jnp.int32)
    own_tile = row_ids // tile_size
    select = (own_tile[:, None] == jnp.arange(pattern_rows.shape[0], dtype=jnp.int32)[None, :]).astype(jnp.float32)
    keep_mask = product(select, pattern_rows.astype(jnp.float32))
    keep_mask = jnp.repeat(keep_mask, tile_size, axis=1)
    return product(panel_rows * keep_mask, inverse.T)


def extend_rows(panel_t, tile_map, row_ids, tile_size):
    parent_tile = row_ids // tile_size
    matches = parent_tile[:, None] == tile_map[None, :]
    present = jnp.sum(matches.astype(jnp.int32), axis=1)
    positions = jnp.arange(tile_map.shape[0], dtype=jnp.int32)[None, :]
    source_tile = jnp.sum(jnp.where(matches, positions, jnp.zeros_like(positions)), axis=1)
    source = (source_tile * tile_size + row_ids % tile_size).astype(jnp.int32)
    picked = jnp.take(panel_t, source, axis=0)
    return jnp.where(present[:, None] > 0, picked, jnp.zeros_like(picked))


def reference(panel, pattern, child_inverse, ext_map, upper_rows, parent_inverse, update_block):
    blocks = []
    all_rows = jnp.arange(PP + MP, dtype=jnp.int32)
    for parent in range(N_CUBE // 2):
        even_child = 2 * parent
        odd_child = 2 * parent + 1
        even_wt = child_rows(panel[even_child], pattern[even_child], child_inverse[even_child], 0, TILE)
        odd_wt = child_rows(panel[odd_child], pattern[odd_child], child_inverse[odd_child], 0, TILE)
        front = jnp.concatenate([extend_rows(even_wt, ext_map[even_child], all_rows, TILE),
                                 extend_rows(odd_wt, ext_map[odd_child], all_rows, TILE)], axis=1)
        front_pivot = front[:PP]
        front_update = front[PP:]
        upper_full = jnp.concatenate([upper_rows[even_child], upper_rows[odd_child]], axis=0)
        pivot_inv = jnp.concatenate([parent_inverse[even_child], parent_inverse[odd_child]], axis=0)
        upper_hat = upper_full - product(front_update, front_pivot.T)
        parent_wt = product(upper_hat, pivot_inv.T)
        update_full = jnp.concatenate([update_block[even_child], update_block[odd_child]], axis=0)
        schur_full = update_full - product(front_update, front_update.T) - product(parent_wt, parent_wt.T)
        blocks.append(schur_full[:MP // 2])
        blocks.append(schur_full[MP // 2:])
    return jnp.stack(blocks)
```

```python
import jax
import jax.numpy as jnp
from jax import lax
from jax.experimental import pallas as pl
from jax.experimental.pallas import tpu as pltpu
from jax.sharding import PartitionSpec as P

MESH = pl.DeviceIdType.MESH
F32 = jnp.float32
BF16 = jnp.bfloat16
NX, NZ = 4, 8
ROWS = 64
TILE = 256


def nt(left, right):
    return lax.dot_general(left, right, (((1,), (1,)), ((), ())), preferred_element_type=F32)


def nn(left, right):
    return lax.dot_general(left, right, (((1,), (0,)), ((), ())), preferred_element_type=F32)


def split(value):
    high = value.astype(BF16)
    return high, (value - high.astype(F32)).astype(BF16)


def stack(value):
    return jnp.concatenate(split(value), axis=0)


def dot3(mul, left, right_high, right_low):
    count = left.shape[0]
    both = stack(left)
    wide = mul(both, right_high)
    return wide[:count] + wide[count:] + mul(both[:count], right_low)


class Wires:
    def __init__(self, send_sems, recv_sems, any_device):
        self.send_sems, self.recv_sems, self.any_device = send_sems, recv_sems, any_device
        self.number, self.started = {}, []

    def copy(self, name, source, target, device):
        index = self.number.setdefault(name, len(self.number))
        return pltpu.make_async_remote_copy(
            src_ref=source,
            dst_ref=target,
            send_sem=self.send_sems.at[index],
            recv_sem=self.recv_sems.at[index],
            device_id=device,
            device_id_type=MESH,
        )

    def send(self, name, source, target, device):
        copy = self.copy(name, source, target, device)
        copy.start()
        self.started.append(copy)

    def arrive(self, name, target):
        self.copy(name, target, target, self.any_device).wait_recv()

    def drain(self):
        for copy in self.started:
            copy.wait_send()


def kernel(
    ext_ref, pat_ref, panel_ref, cinv_ref, upper_ref, pinv_ref, block_ref, out_ref,
    cbuf, ubuf, ucols, gbuf, panel_v, cinv_v, block_v, out_v,
    p_high, p_low, g_high, g_low, b_cat, y_cat, local_sems, out_sems, send_sems, recv_sems,
):
    cube, grid = lax.axis_index("cube"), lax.axis_index("grid")
    y, low = cube // 2, cube % 2
    high, z, core = grid // 16, (grid % 16) // 2, grid % 2
    x = high * 2 + low

    def device(xx, zz, cc):
        return (y * 2 + xx % 2, (xx // 2) * 16 + zz * 2 + cc)

    sibling = device(x, z, 1 - core)
    x_next = {1: device((x + 1) % NX, z, core), -1: device((x + 3) % NX, z, core)}
    x_far = device((x + 2) % NX, z, core)
    z_next = {1: device(x, (z + 1) % NZ, core), -1: device(x, (z + 7) % NZ, core)}

    def rows_of(xx, zz, cc, first, count):
        tile = (xx // 2) * 4 + zz // 2
        start = pl.multiple_of((zz % 2) * 128 + cc * ROWS + first, 8)
        return tile, pl.ds(start, count)

    def c_slot(dx, dz, cc, first=0, count=ROWS):
        xx, zz = (x + dx + NX) % NX, (z + dz + NZ) % NZ
        tile, rows = rows_of(xx, zz, cc, first, count)
        return cbuf.at[xx % 2, tile, rows]

    def u_slot(dx, dz, cc, first=0, count=ROWS):
        xx, zz = (x + dx + NX) % NX, (z + dz + NZ) % NZ
        tile, rows = rows_of(xx, zz, cc, first, count)
        return ubuf.at[tile, rows]

    loads = [
        pltpu.make_async_copy(panel_ref.at[0], panel_v, local_sems.at[0]),
        pltpu.make_async_copy(cinv_ref.at[0], cinv_v, local_sems.at[1]),
        pltpu.make_async_copy(upper_ref.at[0], u_slot(0, 0, core), local_sems.at[2]),
        pltpu.make_async_copy(
            pinv_ref.at[0], gbuf.at[pl.ds(pl.multiple_of(low * 256, 256), 256)], local_sems.at[3]
        ),
        pltpu.make_async_copy(block_ref.at[0], block_v, local_sems.at[4]),
    ]
    for load in loads:
        load.start()

    barrier = pltpu.get_barrier_semaphore()
    greeted = [sibling, x_next[1], x_next[-1], x_far, z_next[1], z_next[-1]]
    for other in greeted:
        pl.semaphore_signal(barrier, inc=1, device_id=other, device_id_type=MESH)
    pl.semaphore_wait(barrier, len(greeted))

    wires = Wires(send_sems, recv_sems, sibling)

    loads[2].wait()
    own_u = u_slot(0, 0, core)
    wires.send(("u", "far"), own_u, own_u, x_far)
    for way in (1, -1):
        wires.send(("u", 0, way, 1), own_u, own_u, z_next[way])
    wires.send(("u", "own", "pair"), own_u, own_u, sibling)

    loads[3].wait()

    def g_rows(half, way, cc):
        start = half * 256 + (0 if way == 1 else 128) + cc * 64
        return gbuf.at[pl.ds(pl.multiple_of(start, 64), 64)]

    for way in (1, -1):
        wires.send(("g", way), g_rows(low, way, core), g_rows(low, way, core), x_next[way])

    loads[0].wait()
    loads[1].wait()
    own_tile = grid // 4
    keep = [pat_ref[0, own_tile, part].astype(F32) for part in range(2)]
    masked = jnp.concatenate([panel_v[:, :256] * keep[0], panel_v[:, 256:] * keep[1]], axis=1)
    inv_high, inv_low = split(cinv_v[...])
    tile, rows = rows_of(x, z, core, 0, ROWS)
    cbuf[low, tile, rows, :] = dot3(nt, masked, inv_high, inv_low)

    half = ROWS // 2

    def span(step, way):
        if step < NZ // 2:
            return 0, ROWS
        return (0, half) if way == 1 else (half, half)

    def c_start_x(step, way):
        first, count = span(step, way)
        piece = c_slot(0, -way * step, core, first, count)
        for side in (1, -1):
            wires.send(("c", step, way, "x", side), piece, piece, x_next[side])

    def c_pair(name, piece):
        wires.send(name + ("pair",), piece, piece, sibling)

    def c_mid_x(step, way):
        first, count = span(step, way)
        for side in (1, -1):
            piece = c_slot(-side, -way * step, core, first, count)
            wires.arrive(("c", step, way, "x", side), piece)
            part = c_slot(-side, -way * step, core, first + (0 if side == 1 else count // 2), count // 2)
            wires.send(("c", step, way, "xx", side), part, part, x_next[side])
            c_pair(("c", step, way, "x", side), piece)

    def c_end_x(step, way):
        first, count = span(step, way)
        for side in (1, -1):
            part = c_slot(2, -way * step, core, first + (0 if side == 1 else count // 2), count // 2)
            wires.arrive(("c", step, way, "xx", side), part)
            c_pair(("c", step, way, "xx", side), part)

    def ring(kind, slot, step, way):
        first, count = span(step, way)
        piece = slot(-way * step, first, count)
        wires.arrive(kind + (way, step), piece)
        if step < NZ // 2:
            first, count = span(step + 1, way)
            part = slot(-way * step, first, count)
            wires.send(kind + (way, step + 1), part, part, z_next[way])
        wires.send(kind + (way, step, "pair"), piece, piece, sibling)

    def u_ring(dx, step, way):
        ring(("u", dx), lambda dz, first, count: u_slot(dx, dz, core, first, count), step, way)

    own_c = c_slot(0, 0, core)
    c_start_x(0, 1)
    for way in (1, -1):
        wires.send(("c", "z", way, 1), own_c, own_c, z_next[way])
    wires.send(("c", "own", "pair"), own_c, own_c, sibling)

    far_u = u_slot(2, 0, core)
    wires.arrive(("u", "far"), far_u)
    for way in (1, -1):
        wires.send(("u", 2, way, 1), far_u, far_u, z_next[way])
    wires.send(("u", "far", "pair"), far_u, far_u, sibling)
    for way in (1, -1):
        wires.arrive(("g", way), g_rows(1 - low, way, core))
        wires.send(("g", way, "pair"), g_rows(1 - low, way, core), g_rows(1 - low, way, core), sibling)

    rounds = [[(0, 1)]] + [[(step, 1), (step, -1)] for step in range(1, NZ // 2 + 1)]
    for step in range(1, len(rounds) + 2):
        if step < len(rounds):
            for _, way in rounds[step]:
                ring(("c", "z"), lambda dz, first, count: c_slot(0, dz, core, first, count), step, way)
                c_start_x(step, way)
            for _, way in rounds[step]:
                u_ring(0, step, way)
        if step - 1 < len(rounds):
            for pair in rounds[step - 1]:
                c_mid_x(*pair)
        if step < len(rounds):
            for _, way in rounds[step]:
                u_ring(2, step, way)
        if 0 <= step - 2 < len(rounds):
            for pair in rounds[step - 2]:
                c_end_x(*pair)

    other = 1 - core
    wires.arrive(("u", "own", "pair"), u_slot(0, 0, other))
    wires.arrive(("u", "far", "pair"), u_slot(2, 0, other))
    for dx in (0, 2):
        for step in range(1, NZ // 2 + 1):
            for way in (1, -1):
                wires.arrive(("u", dx, way, step, "pair"), u_slot(dx, -way * step, other, *span(step, way)))

    column_tile = high * 4 * 2 + z
    own_cols = low == high
    inner = jnp.logical_not(own_cols)
    tile_in_half = z
    col_rows = pl.multiple_of(core * 128, 128)

    @pl.when(own_cols)
    def _():
        ucols[...] = ubuf[tile_in_half, pl.ds(col_rows, 128), :]

    def cols_copy(way):
        first = 0 if way == 1 else ROWS
        return wires.copy(
            ("cols", way),
            ubuf.at[tile_in_half, pl.ds(pl.multiple_of(col_rows + first, 64), ROWS)],
            ucols.at[pl.ds(first, ROWS)],
            x_next[way],
        )

    def cols_needed(xx):
        return jnp.logical_or(xx == 1, xx == 2)

    for way in (1, -1):
        @pl.when(cols_needed((x + way + NX) % NX))
        def _(way=way):
            cols_copy(way).start()

    for way in (1, -1):
        wires.arrive(("g", way, "pair"), g_rows(1 - low, way, other))

    wires.arrive(("c", "own", "pair"), c_slot(0, 0, other))
    for step in range(1, NZ // 2 + 1):
        for way in (1, -1):
            wires.arrive(("c", "z", way, step, "pair"), c_slot(0, -way * step, other, *span(step, way)))
    for pairs in rounds:
        for step, way in pairs:
            first, count = span(step, way)
            for side in (1, -1):
                wires.arrive(
                    ("c", step, way, "x", side, "pair"), c_slot(-side, -way * step, other, first, count)
                )
                part = c_slot(2, -way * step, other, first + (0 if side == 1 else count // 2), count // 2)
                wires.arrive(("c", step, way, "xx", side, "pair"), part)

    for way in (1, -1):
        @pl.when(inner)
        def _(way=way):
            first = 0 if way == 1 else ROWS
            wires.arrive(("cols", way), ucols.at[pl.ds(first, ROWS)])

    def source(child, parent_tile):
        row = y * 2 + child
        where, found = jnp.int32(0), jnp.int32(0)
        for position in range(8):
            hit = (ext_ref[row, position] == parent_tile).astype(jnp.int32)
            where, found = jnp.where(hit > 0, position, where), found + hit
        return where, found.astype(F32)

    g_high[...], g_low[...] = split(gbuf[...])
    columns = []
    for child in range(2):
        where, found = source(child, 2 + column_tile)
        columns.append(cbuf[child, where, pl.ds(col_rows, 128), :] * found)
        for pivot in range(2):
            where, found = source(child, jnp.int32(pivot))
            p_high[pivot, child], p_low[pivot, child] = split(cbuf[child, where] * found)
    hat = []
    for pivot in range(2):
        part = ucols[:, pivot * 256 : (pivot + 1) * 256]
        for child in range(2):
            part = part - dot3(nt, columns[child], p_high[pivot, child], p_low[pivot, child])
        hat.append(part)
    weight = dot3(nt, jnp.concatenate(hat, axis=1), g_high[...], g_low[...])
    back = dot3(nn, weight, g_high[...], g_low[...])
    y_cat[...] = stack(back)
    for child in range(2):
        total = columns[child]
        for pivot in range(2):
            total = total - dot3(
                nn, back[:, pivot * 256 : (pivot + 1) * 256], p_high[pivot, child], p_low[pivot, child]
            )
        b_cat[child] = stack(total)

    loads[4].wait()

    def times(value, right):
        value_high, value_low = split(value)
        wide = nt(value_high, right)
        return wide[:, :128] + wide[:, 128:] + nt(value_low, right[:128])

    for index in range(8):
        total = block_v[pl.ds(index * TILE, TILE), :] - times(ubuf[index], y_cat[...])
        for child in range(2):
            where, found = source(child, 2 + low * 8 + index)
            total = total - times(cbuf[child, where], b_cat[child]) * found
        out_v[pl.ds(index * TILE, TILE), :] = total
        pltpu.make_async_copy(
            out_v.at[pl.ds(index * TILE, TILE)], out_ref.at[0, pl.ds(index * TILE, TILE)], out_sems.at[index]
        ).start()

    wires.drain()
    for way in (1, -1):
        @pl.when(cols_needed((x + way + NX) % NX))
        def _(way=way):
            cols_copy(way).wait_send()
    for index in range(8):
        pltpu.make_async_copy(
            out_v.at[pl.ds(index * TILE, TILE)], out_ref.at[0, pl.ds(index * TILE, TILE)], out_sems.at[index]
        ).wait()


def local(panel, pattern, child_inverse, ext_map, upper_rows, parent_inverse, update_block):
    smem = pl.BlockSpec(memory_space=pltpu.SMEM)
    anywhere = pl.BlockSpec(memory_space=pl.ANY)
    return pl.pallas_call(
        kernel,
        out_shape=jax.ShapeDtypeStruct((1, 2048, 128), F32),
        in_specs=[smem, smem] + [anywhere] * 5,
        out_specs=anywhere,
        scratch_shapes=[
            pltpu.VMEM((2, 8, TILE, 512), F32),
            pltpu.VMEM((8, TILE, 512), F32),
            pltpu.VMEM((128, 512), F32),
            pltpu.VMEM((512, 512), F32),
            pltpu.VMEM((ROWS, 512), F32),
            pltpu.VMEM((512, 512), F32),
            pltpu.VMEM((2048, 128), F32),
            pltpu.VMEM((2048, 128), F32),
            pltpu.VMEM((2, 2, TILE, 512), BF16),
            pltpu.VMEM((2, 2, TILE, 512), BF16),
            pltpu.VMEM((512, 512), BF16),
            pltpu.VMEM((512, 512), BF16),
            pltpu.VMEM((2, 256, 512), BF16),
            pltpu.VMEM((256, 512), BF16),
            pltpu.SemaphoreType.DMA((5,)),
            pltpu.SemaphoreType.DMA((8,)),
            pltpu.SemaphoreType.DMA((160,)),
            pltpu.SemaphoreType.DMA((160,)),
        ],
        compiler_params=pltpu.CompilerParams(
            collective_id=0, has_side_effects=True, vmem_limit_bytes=52 * 2**20
        ),
    )(ext_map, pattern, panel, child_inverse, upper_rows, parent_inverse, update_block)


def solution(mesh):
    in_specs = (
        P("cube", "grid", None),
        P("cube", None, None),
        P("cube", None, None),
        P(),
        P("cube", "grid", None),
        P("cube", None, None),
        P("cube", None, "grid"),
    )
    out_specs = P("cube", None, "grid")
    return jax.shard_map(local, mesh=mesh, in_specs=in_specs, out_specs=out_specs, check_vma=False)
```

```python
import jax
import jax.numpy as jnp
from jax import lax
from jax.experimental import pallas as pl
from jax.experimental.pallas import tpu as pltpu
from jax.sharding import PartitionSpec as P

MESH = pl.DeviceIdType.MESH
F32 = jnp.float32
BF16 = jnp.bfloat16
NX, NZ = 4, 8
ROWS = 64
CUT = 48
WEIGHT = {"a": 0.0, "b": -4.0, "u": 0.0, "g": 0.0, "cols": 0.0}
TILE = 256


def nt(left, right):
    return lax.dot_general(left, right, (((1,), (1,)), ((), ())), preferred_element_type=F32)


def nn(left, right):
    return lax.dot_general(left, right, (((1,), (0,)), ((), ())), preferred_element_type=F32)


def split(value):
    high = value.astype(BF16)
    return high, (value - high.astype(F32)).astype(BF16)


def stack(value):
    return jnp.concatenate(split(value), axis=0)


def dot3(mul, left, right_high, right_low):
    count = left.shape[0]
    both = stack(left)
    wide = mul(both, right_high)
    return wide[:count] + wide[count:] + mul(both[:count], right_low)


WAYS = (1, -1)
LAST = NZ // 2
TAIL = ROWS - CUT
ROW_TIME, LATENCY, AHEAD, STEP = 0.0415, 2.0, 2.5, 0.05


def span(first, count, step, way):
    if step < LAST:
        return first, count
    return (first, count // 2) if way == 1 else (first + count // 2, count // 2)


def part(first, count, side, way):
    front = (count // 2 + (4 if way == 1 else 0)) // 8 * 8
    return (first, front) if side == 1 else (first + front, count - front)


def messages():
    table, after = {}, {}

    def add(name, links, count, *needs):
        table[name], after[name] = (links, count), needs

    def ring(base, needs, first, count):
        for way in WAYS:
            before = needs
            for step in range(1, LAST + 1):
                add(base + (way, step), (("z", way),), span(first, count, step, way)[1], *before)
                before = (base + (way, step),)

    ring(("a", "z"), ("C",), 0, CUT)
    for step in range(LAST + 1):
        for way in WAYS if step else (1,):
            first, count = span(0, CUT, step, way)
            for side in WAYS:
                near = ("a", step, way, "x", side)
                add(near, (("x", side),), count, ("a", "z", way, step) if step else "C")
                add(near[:3] + ("xx", side), (("x", side),), part(first, count, side, way)[1], near)
    ring(("b", 0), ("C",), CUT, TAIL)
    for side in WAYS:
        add(("b", "x", side), (("x", side),), TAIL, "C")
        add(("b", "xx", side), (("x", side),), part(CUT, TAIL, side, 1)[1], ("b", "x", side))
        ring(("b", -side), (("b", "x", side),), CUT, TAIL)
    ring(("b", 2), (("b", "xx", 1), ("b", "xx", -1)), CUT, TAIL)
    ring(("u", 0), ("U",), 0, ROWS)
    add(("u", "far"), (("x", 1), ("x", -1)), ROWS, "U")
    ring(("u", 2), (("u", "far"),), 0, ROWS)
    rows_of_u = tuple(name for name in table if name[0] == "u")
    for side in WAYS:
        add(("g", side), (("x", side),), ROWS, "G")
        add(("cols", side), (("x", side),), ROWS, *rows_of_u)
    return table, after


def plan():
    table, after = messages()
    users = {}
    for name, needs in after.items():
        for need in needs:
            users.setdefault(need, []).append(name)
    chain = {}

    def length(name):
        if name not in chain:
            chain[name] = max(
                (length(user) + LATENCY + table[user][1] * ROW_TIME for user in users.get(name, ())), default=0.0
            )
        return chain[name]

    def rank(name):
        return length(name) + WEIGHT[name[0]]

    links = [(axis, way) for axis in "xz" for way in WAYS]
    free = {link: 0.0 for link in links}
    ready = []
    missing = {name: len(needs) for name, needs in after.items()}
    now, events, order = 0.0, [(0.0, 0, "U"), (0.0, 1, "C"), (0.0, 2, "G")], []
    number = 3
    while events:
        events.sort()
        time, _, name = events.pop(0)
        now = max(now, time) + 2 * STEP
        order.append(("wait", name))
        for user in users.get(name, ()):
            missing[user] -= 1
            if not missing[user]:
                ready.append(user)
        ready.sort(key=lambda user: -rank(user))
        for user in list(ready):
            over, count = table[user]
            if max(free[link] for link in over) - now > AHEAD:
                continue
            ready.remove(user)
            end = max([now] + [free[link] for link in over]) + count * ROW_TIME
            for link in over:
                free[link] = end
            events.append((end + LATENCY, number, user))
            number += 1
            order.append(("send", user))
            now += STEP
    assert not ready
    return order


class Wires:
    def __init__(self, send_sems, recv_sems, pair_sems, model, any_device):
        self.send_sems, self.recv_sems, self.pair_sems = send_sems, recv_sems, pair_sems
        self.model, self.any_device = model, any_device
        self.number, self.sent, self.paired = {}, {}, {}

    def copy(self, source, target, send_sem, recv_sem, device):
        return pltpu.make_async_remote_copy(
            src_ref=source,
            dst_ref=target,
            send_sem=send_sem,
            recv_sem=recv_sem,
            device_id=device,
            device_id_type=MESH,
        )

    def named(self, name):
        return self.recv_sems.at[self.number.setdefault(name, len(self.number))]

    def send(self, name, piece, device):
        self.copy(piece, piece, self.send_sems.at[0], self.named(name), device).start()
        self.sent[0] = self.sent.get(0, 0) + piece.shape[0]

    def arrive(self, name, piece):
        self.copy(piece, piece, self.send_sems.at[0], self.named(name), self.any_device).wait_recv()

    def pair(self, kind, piece):
        self.copy(piece, piece, self.send_sems.at[1], self.pair_sems.at[kind], self.any_device).start()
        self.sent[1] = self.sent.get(1, 0) + piece.shape[0]
        self.paired[kind] = self.paired.get(kind, 0) + piece.shape[0]

    def rows(self, count):
        for outer in (1, 2):
            for tiles in range(1, 9):
                if count % (outer * tiles * 8) == 0 and count // (outer * tiles) <= TILE:
                    return self.model.at[pl.ds(0, outer), pl.ds(0, tiles), pl.ds(0, count // (outer * tiles))]
        raise ValueError(count)

    def pair_arrive(self, kind):
        piece = self.rows(self.paired[kind])
        self.copy(piece, piece, self.send_sems.at[1], self.pair_sems.at[kind], self.any_device).wait_recv()

    def drain(self):
        for kind, count in self.sent.items():
            piece = self.rows(count)
            self.copy(piece, piece, self.send_sems.at[kind], self.pair_sems.at[0], self.any_device).wait_send()


def kernel(
    ext_hbm, pat_hbm, panel_ref, cinv_ref, upper_ref, pinv_ref, block_ref, out_ref,
    cbuf, ubuf, ucols, gbuf, panel_v, cinv_v, block_v,
    p_high, p_low, g_high, g_low, b_cat, y_cat, ext_ref, pat_ref,
    local_sems, send_sems, recv_sems, pair_sems, cols_sems,
):
    cube, grid = lax.axis_index("cube"), lax.axis_index("grid")
    y, low = cube // 2, cube % 2
    high, z, core = grid // 16, (grid % 16) // 2, grid % 2
    x = high * 2 + low

    def device(xx, zz, cc):
        return (y * 2 + xx % 2, (xx // 2) * 16 + zz * 2 + cc)

    sibling = device(x, z, 1 - core)
    x_next = {1: device((x + 1) % NX, z, core), -1: device((x + 3) % NX, z, core)}
    x_far = device((x + 2) % NX, z, core)
    z_next = {1: device(x, (z + 1) % NZ, core), -1: device(x, (z + 7) % NZ, core)}

    def rows_of(xx, zz, cc, first, count):
        tile = (xx // 2) * 4 + zz // 2
        start = pl.multiple_of((zz % 2) * 128 + cc * ROWS + first, 8)
        return tile, pl.ds(start, count)

    def c_slot(dx, dz, cc, first=0, count=ROWS):
        xx, zz = (x + dx + NX) % NX, (z + dz + NZ) % NZ
        tile, rows = rows_of(xx, zz, cc, first, count)
        return cbuf.at[xx % 2, tile, rows]

    def u_slot(dx, dz, cc, first=0, count=ROWS):
        xx, zz = (x + dx + NX) % NX, (z + dz + NZ) % NZ
        tile, rows = rows_of(xx, zz, cc, first, count)
        return ubuf.at[tile, rows]

    loads = [
        pltpu.make_async_copy(panel_ref.at[0], panel_v, local_sems.at[0]),
        pltpu.make_async_copy(cinv_ref.at[0], cinv_v, local_sems.at[1]),
        pltpu.make_async_copy(upper_ref.at[0], u_slot(0, 0, core), local_sems.at[2]),
        pltpu.make_async_copy(
            pinv_ref.at[0], gbuf.at[pl.ds(pl.multiple_of(low * 256, 256), 256)], local_sems.at[3]
        ),
        pltpu.make_async_copy(block_ref.at[0], block_v, local_sems.at[4]),
        pltpu.make_async_copy(pat_hbm, pat_ref, local_sems.at[5]),
        pltpu.make_async_copy(ext_hbm, ext_ref, local_sems.at[6]),
    ]
    for load in loads:
        load.start()

    barrier = pltpu.get_barrier_semaphore()
    greeted = [sibling, x_next[1], x_next[-1], x_far, z_next[1], z_next[-1]]
    for other in greeted:
        pl.semaphore_signal(barrier, inc=1, device_id=other, device_id_type=MESH)

    wires = Wires(send_sems, recv_sems, pair_sems, cbuf, sibling)
    def c_at(dx):
        return lambda dz, first, count: c_slot(dx, dz, core, first, count)

    def u_at(dx):
        return lambda dz, first, count: u_slot(dx, dz, core, first, count)

    def g_rows(half, way):
        start = half * 256 + (0 if way == 1 else 128) + core * 64
        return gbuf.at[pl.ds(pl.multiple_of(start, 64), 64)]

    def arrived(name):
        kind = name[0]
        if kind == "g":
            return g_rows(1 - low, name[1])
        if kind == "u":
            if name[1] == "far":
                return u_slot(2, 0, core)
            _, dx, way, step = name
            return u_slot(dx, -way * step, core, *span(0, ROWS, step, way))
        if kind == "a" and name[1] == "z":
            _, _, way, step = name
            return c_slot(0, -way * step, core, *span(0, CUT, step, way))
        if kind == "a":
            _, step, way, reach, side = name
            rows = span(0, CUT, step, way)
            if reach == "x":
                return c_slot(-side, -way * step, core, *rows)
            return c_slot(2, -way * step, core, *part(*rows, side, way))
        if name[1] == "x":
            return c_slot(-name[2], 0, core, CUT, TAIL)
        if name[1] == "xx":
            return c_slot(2, 0, core, *part(CUT, TAIL, name[2], 1))
        _, dx, way, step = name
        return c_slot(dx, -way * step, core, *span(CUT, TAIL, step, way))

    def leaving(name):
        kind = name[0]
        if kind == "g":
            return g_rows(low, name[1]), x_next[name[1]]
        if kind == "u":
            if name[1] == "far":
                return u_slot(0, 0, core), x_far
            _, dx, way, step = name
            return u_slot(dx, -way * (step - 1), core, *span(0, ROWS, step, way)), z_next[way]
        if kind == "a" and name[1] == "z":
            _, _, way, step = name
            return c_slot(0, -way * (step - 1), core, *span(0, CUT, step, way)), z_next[way]
        if kind == "a":
            _, step, way, reach, side = name
            rows = span(0, CUT, step, way)
            if reach == "x":
                return c_slot(0, -way * step, core, *rows), x_next[side]
            return c_slot(-side, -way * step, core, *part(*rows, side, way)), x_next[side]
        if name[1] == "x":
            return c_slot(0, 0, core, CUT, TAIL), x_next[name[2]]
        if name[1] == "xx":
            return c_slot(-name[2], 0, core, *part(CUT, TAIL, name[2], 1)), x_next[name[2]]
        _, dx, way, step = name
        return c_slot(dx, -way * (step - 1), core, *span(CUT, TAIL, step, way)), z_next[way]

    column_tile = high * 8 + z
    own_cols = low == high
    inner = jnp.logical_not(own_cols)
    col_rows = pl.multiple_of(core * 128, 128)

    def cols_copy(way):
        first = 0 if way == 1 else ROWS
        return wires.copy(
            ubuf.at[z, pl.ds(pl.multiple_of(col_rows + first, 64), ROWS)],
            ucols.at[pl.ds(first, ROWS)],
            cols_sems.at[0, 0 if way == 1 else 1],
            cols_sems.at[1, 0 if way == 1 else 1],
            x_next[way],
        )

    def cols_when(way):
        beside = (x + way + NX) % NX
        return pl.when(jnp.logical_or(beside == 1, beside == 2))

    loads[0].wait()
    loads[1].wait()
    loads[5].wait()
    own_tile = grid // 4
    keep = [pat_ref[0, side, own_tile].astype(F32) for side in range(2)]
    masked = jnp.concatenate([panel_v[:, :256] * keep[0], panel_v[:, 256:] * keep[1]], axis=1)
    inv_high, inv_low = split(cinv_v[...])
    tile, rows = rows_of(x, z, core, 0, ROWS)
    cbuf[low, tile, rows, :] = dot3(nt, masked, inv_high, inv_low)
    loads[2].wait()
    loads[3].wait()

    pl.semaphore_wait(barrier, len(greeted))

    pair_kind = {"a": 0, "b": 0, "u": 1, "g": 2}
    for action, name in plan():
        if action == "wait":
            if name == "U":
                wires.pair(1, u_slot(0, 0, core))
            elif name == "C":
                wires.pair(0, c_slot(0, 0, core))
            elif name[0] in pair_kind:
                piece = arrived(name)
                wires.arrive(name, piece)
                wires.pair(pair_kind[name[0]], piece)
        elif name[0] == "cols":
            if name[1] == 1:
                wires.pair_arrive(1)

                @pl.when(own_cols)
                def _():
                    ucols[...] = ubuf[z, pl.ds(col_rows, 128), :]

            @cols_when(name[1])
            def _(way=name[1]):
                cols_copy(way).start()
        else:
            wires.send(name, *leaving(name))

    wires.pair_arrive(2)
    wires.pair_arrive(0)
    for way in WAYS:
        @pl.when(inner)
        def _(way=way):
            cols_copy(way).wait_recv()

    loads[6].wait()

    def source(child, parent_tile):
        row = y * 2 + child
        where, found = jnp.int32(0), jnp.int32(0)
        for position in range(8):
            hit = (ext_ref[row, position] == parent_tile).astype(jnp.int32)
            where, found = jnp.where(hit > 0, position, where), found + hit
        return where, found.astype(F32)

    g_high[...], g_low[...] = split(gbuf[...])
    columns = []
    for child in range(2):
        where, found = source(child, 2 + column_tile)
        columns.append(cbuf[child, where, pl.ds(col_rows, 128), :] * found)
        for pivot in range(2):
            where, found = source(child, jnp.int32(pivot))
            p_high[pivot, child], p_low[pivot, child] = split(cbuf[child, where] * found)
    hat = []
    for pivot in range(2):
        minus = ucols[:, pivot * 256 : (pivot + 1) * 256]
        for child in range(2):
            minus = minus - dot3(nt, columns[child], p_high[pivot, child], p_low[pivot, child])
        hat.append(minus)
    weight = dot3(nt, jnp.concatenate(hat, axis=1), g_high[...], g_low[...])
    back = dot3(nn, weight, g_high[...], g_low[...])
    y_cat[...] = stack(back)
    for child in range(2):
        total = columns[child]
        for pivot in range(2):
            total = total - dot3(
                nn, back[:, pivot * 256 : (pivot + 1) * 256], p_high[pivot, child], p_low[pivot, child]
            )
        b_cat[child] = stack(total)

    loads[4].wait()

    def times(value, right):
        value_high, value_low = split(value)
        wide = nt(value_high, right)
        return wide[:, :128] + wide[:, 128:] + nt(value_low, right[:128])

    for index in range(8):
        total = block_v[pl.ds(index * TILE, TILE), :] - times(ubuf[index], y_cat[...])
        for child in range(2):
            where, found = source(child, 2 + low * 8 + index)
            total = total - times(cbuf[child, where], b_cat[child]) * found
        out_ref[0, pl.ds(index * TILE, TILE), :] = total

    wires.drain()
    for way in WAYS:
        @cols_when(way)
        def _(way=way):
            cols_copy(way).wait_send()


def local(panel, pattern, child_inverse, ext_map, upper_rows, parent_inverse, update_block):
    anywhere = pl.BlockSpec(memory_space=pltpu.HBM)
    return pl.pallas_call(
        kernel,
        out_shape=pltpu.VMEM((1, 2048, 128), F32),
        in_specs=[anywhere] * 7,
        out_specs=pl.BlockSpec(memory_space=pltpu.VMEM),
        scratch_shapes=[
            pltpu.VMEM((2, 8, TILE, 512), F32),
            pltpu.VMEM((8, TILE, 512), F32),
            pltpu.VMEM((128, 512), F32),
            pltpu.VMEM((512, 512), F32),
            pltpu.VMEM((ROWS, 512), F32),
            pltpu.VMEM((512, 512), F32),
            pltpu.VMEM((2048, 128), F32),
            pltpu.VMEM((2, 2, TILE, 512), BF16),
            pltpu.VMEM((2, 2, TILE, 512), BF16),
            pltpu.VMEM((512, 512), BF16),
            pltpu.VMEM((512, 512), BF16),
            pltpu.VMEM((2, 256, 512), BF16),
            pltpu.VMEM((256, 512), BF16),
            pltpu.SMEM((8, 8), jnp.int32),
            pltpu.SMEM((1, 2, 8), jnp.int32),
            pltpu.SemaphoreType.DMA((7,)),
            pltpu.SemaphoreType.DMA((2,)),
            pltpu.SemaphoreType.DMA((103,)),
            pltpu.SemaphoreType.DMA((3,)),
            pltpu.SemaphoreType.DMA((2, 2)),
        ],
        compiler_params=pltpu.CompilerParams(
            collective_id=0, has_side_effects=True, vmem_limit_bytes=60 * 2**20
        ),
    )(ext_map, jnp.swapaxes(pattern, 1, 2), panel, child_inverse, upper_rows, parent_inverse, update_block)


def solution(mesh):
    in_specs = (
        P("cube", "grid", None),
        P("cube", None, None),
        P("cube", None, None),
        P(),
        P("cube", "grid", None),
        P("cube", None, None),
        P("cube", None, "grid"),
    )
    out_specs = P("cube", None, "grid")
    return jax.shard_map(local, mesh=mesh, in_specs=in_specs, out_specs=out_specs, check_vma=False)
```

```python
import math

import jax
import jax.numpy as jnp
from jax import lax
from jax.experimental import pallas as pl
from jax.experimental.pallas import tpu as pltpu
from jax.sharding import PartitionSpec as P

MESH = pl.DeviceIdType.MESH
F32 = jnp.float32
BF16 = jnp.bfloat16
NX, NZ = 4, 8
ROWS = 64
CUT = 48
TILE = 256


def nt(left, right):
    return lax.dot_general(left, right, (((1,), (1,)), ((), ())), preferred_element_type=F32)


def nn(left, right):
    return lax.dot_general(left, right, (((1,), (0,)), ((), ())), preferred_element_type=F32)


def split(value):
    high = value.astype(BF16)
    return high, (value - high.astype(F32)).astype(BF16)


def stack(value):
    return jnp.concatenate(split(value), axis=0)


def dot3(mul, left, right_high, right_low):
    count = left.shape[0]
    both = stack(left)
    wide = mul(both, right_high)
    return wide[:count] + wide[count:] + mul(both[:count], right_low)


WAYS = (1, -1)
LAST = NZ // 2
TAIL = ROWS - CUT
ROW_TIME, LATENCY, AHEAD, STEP, READY = 0.043, 2.3, 2.5, 0.08, 2.0
PAIR = 1.0
WEIGHT = {("b", "z"): -4.0}


def span(first, count, step, way):
    if step < LAST:
        return first, count
    return (first, count // 2) if way == 1 else (first + count // 2, count // 2)


def part(first, count, side):
    front = max(count // 24, 1) * 8
    return (first, front) if side == 1 else (first + front, count - front)


def messages():
    table, after = {}, {}

    def add(name, links, count, *needs):
        table[name], after[name] = (links, count), needs

    def ring(base, needs, first, count, times=1):
        for way in WAYS:
            before = needs
            for step in range(1, LAST + 1):
                add(base + (way, step), (("z", way),), span(first, count, step, way)[1] * times, *before)
                before = (base + (way, step),)

    ring(("a", "z"), ("C",), 0, CUT)
    for step in range(LAST + 1):
        for way in WAYS if step else (1,):
            first, count = span(0, CUT, step, way)
            for side in WAYS:
                near = ("a", step, way, "x", side)
                add(near, (("x", side),), count, ("a", "z", way, step) if step else "C")
                add(near[:3] + ("xx", side), (("x", side),), part(first, count, side)[1], near)
    for side in WAYS:
        add(("b", "x", side), (("x", side),), TAIL, "C")
        add(("b", "xx", side), (("x", side),), part(CUT, TAIL, side)[1], ("b", "x", side))
    joined = tuple(("b", reach, side) for reach in ("x", "xx") for side in WAYS)
    ring(("b", "z"), joined, CUT, TAIL, NX)
    ring(("u", 0), ("U",), 0, ROWS)
    add(("u", "far"), (("x", 1), ("x", -1)), ROWS, "U")
    ring(("u", 2), (("u", "far"),), 0, ROWS)
    near_u = tuple(name for name in table if name[:2] == ("u", 0))
    for side in WAYS:
        add(("g", side), (("x", side),), ROWS, "G")
    add(("cols", "near"), (("x", 1),), 2 * ROWS, *near_u)
    return table, after


def work(table):
    def of(*kinds):
        return [name for name in table if name[0] in kinds]

    tasks = [("inverse", of("g"), 0.3), ("pivots", of("a", "b"), 0.5), ("hat", of("cols", "u"), 0.6)]
    tasks += [("weight", (), 0.5), ("back", (), 0.5), ("narrow", (), 0.5)]
    return tasks + [(("tile", index), (), 0.45) for index in range(8)]


def plan():
    table, after = messages()
    tasks, landed = work(table), {}
    users = {}
    for name, needs in after.items():
        for need in needs:
            users.setdefault(need, []).append(name)
    chain = {}

    def length(name):
        if name not in chain:
            chain[name] = max(
                (length(user) + LATENCY + table[user][1] * ROW_TIME for user in users.get(name, ())), default=0.0
            )
        return chain[name]

    def rank(name):
        return length(name) + WEIGHT.get(name[:2], 0.0)

    links = [(axis, way) for axis in "xz" for way in WAYS]
    free = {link: 0.0 for link in links}
    ready = []
    missing = {name: len(needs) for name, needs in after.items()}
    now, events, order = 0.0, [(0.0, 0, "U"), (0.1, 1, "G"), (READY, 2, "C")], []
    number = 3
    while events or tasks:
        events.sort()
        if tasks and all(need in landed for need in tasks[0][1]):
            start = max([0.0] + [landed[need] + PAIR for need in tasks[0][1]])
            if not events or max(start, now) < events[0][0]:
                now = max(start, now) + tasks[0][2]
                order.append(("work", tasks.pop(0)[0]))
                continue
        time, _, name = events.pop(0)
        now = max(now, time) + 2 * STEP
        landed[name] = now
        order.append(("wait", name))
        for user in users.get(name, ()):
            missing[user] -= 1
            if not missing[user]:
                ready.append(user)
        ready.sort(key=lambda user: -rank(user))
        for user in list(ready):
            over, count = table[user]
            if max(free[link] for link in over) - now > AHEAD:
                continue
            ready.remove(user)
            end = max([now] + [free[link] for link in over]) + count * ROW_TIME
            for link in over:
                free[link] = end
            events.append((end + LATENCY, number, user))
            number += 1
            order.append(("send", user))
            now += STEP
    assert not ready
    return order


def rows_in(piece):
    return math.prod(piece.shape[:-1])


class Wires:
    def __init__(self, send_sems, recv_sems, pair_sems, model, any_device):
        self.send_sems, self.recv_sems, self.pair_sems = send_sems, recv_sems, pair_sems
        self.model, self.any_device = model, any_device
        self.number, self.sent, self.paired = {}, {}, {}

    def copy(self, source, target, send_sem, recv_sem, device):
        return pltpu.make_async_remote_copy(
            src_ref=source,
            dst_ref=target,
            send_sem=send_sem,
            recv_sem=recv_sem,
            device_id=device,
            device_id_type=MESH,
        )

    def named(self, name):
        return self.recv_sems.at[self.number.setdefault(name, len(self.number))]

    def send(self, name, piece, device):
        piece, target = piece if isinstance(piece, tuple) else (piece, piece)
        self.copy(piece, target, self.send_sems.at[0], self.named(name), device).start()
        self.sent[0] = self.sent.get(0, 0) + rows_in(piece)

    def arrive(self, name, piece):
        self.copy(piece, piece, self.send_sems.at[0], self.named(name), self.any_device).wait_recv()

    def pair(self, kind, piece):
        self.copy(piece, piece, self.send_sems.at[1], self.pair_sems.at[kind], self.any_device).start()
        self.sent[1] = self.sent.get(1, 0) + rows_in(piece)
        self.paired[kind] = self.paired.get(kind, 0) + rows_in(piece)

    def rows(self, count):
        for tiles in (16, 8, 4, 3, 2, 1):
            if count % (8 * tiles) == 0 and count // tiles <= TILE:
                both, half, line = 2 if tiles > 8 else 1, 2 if tiles > 4 else 1, min(tiles, 4)
                return self.model.at[pl.ds(0, both), pl.ds(0, half), pl.ds(0, line), pl.ds(0, count // tiles)]
        raise ValueError(count)

    def pair_arrive(self, kind):
        piece = self.rows(self.paired[kind])
        self.copy(piece, piece, self.send_sems.at[1], self.pair_sems.at[kind], self.any_device).wait_recv()

    def drain(self):
        for kind, count in self.sent.items():
            piece = self.rows(count)
            self.copy(piece, piece, self.send_sems.at[kind], self.pair_sems.at[0], self.any_device).wait_send()


def kernel(
    ext_hbm, pat_hbm, panel_ref, cinv_ref, upper_ref, pinv_ref, block_ref, out_ref,
    cbuf, ubuf, ucols, fcols, hats, weights, gbuf, panel_v, cinv_v, block_v,
    p_high, p_low, g_high, g_low, b_cat, y_cat, ext_ref, pat_ref,
    local_sems, send_sems, recv_sems, pair_sems, cols_sems,
):
    cube, grid = lax.axis_index("cube"), lax.axis_index("grid")
    y, low = cube // 2, cube % 2
    high, z, core = grid // 16, (grid % 16) // 2, grid % 2
    x = high * 2 + low

    def device(xx, zz, cc):
        return (y * 2 + xx % 2, (xx // 2) * 16 + zz * 2 + cc)

    turn = jnp.where(z < NZ // 2, 1, -1)
    place = jnp.where(z < NZ // 2, x, NX - 1 - x)

    def across(dx):
        return (x + dx * turn + NX) % NX

    sibling = device(x, z, 1 - core)
    x_next = {1: device(across(1), z, core), -1: device(across(-1), z, core)}
    x_cross = {1: device(across(1), z, 1 - core), -1: device(across(-1), z, 1 - core)}
    x_far = device((x + 2) % NX, z, core)
    z_next = {1: device(x, (z + 1) % NZ, core), -1: device(x, (z + 7) % NZ, core)}

    def rows_of(zz, cc, first, count):
        return pl.ds(pl.multiple_of((zz % 2) * 128 + cc * ROWS + first, 8), count)

    def c_slot(dx, dz, cc, first=0, count=ROWS):
        xx, zz = across(dx), (z + dz + NZ) % NZ
        return cbuf.at[xx % 2, xx // 2, zz // 2, rows_of(zz, cc, first, count)]

    def c_line(dz, cc, first, count):
        zz = (z + dz + NZ) % NZ
        return cbuf.at[:, :, zz // 2, rows_of(zz, cc, first, count)]

    def u_slot(far, dz, cc, first=0, count=ROWS):
        zz = (z + dz + NZ) % NZ
        return ubuf.at[1 if far else 0, zz // 2, rows_of(zz, cc, first, count)]

    loads = [
        pltpu.make_async_copy(panel_ref.at[0], panel_v, local_sems.at[0]),
        pltpu.make_async_copy(cinv_ref.at[0], cinv_v, local_sems.at[1]),
        pltpu.make_async_copy(upper_ref.at[0], u_slot(0, 0, core), local_sems.at[2]),
        pltpu.make_async_copy(
            pinv_ref.at[0], gbuf.at[pl.ds(pl.multiple_of(low * 256, 256), 256)], local_sems.at[3]
        ),
        pltpu.make_async_copy(block_ref.at[0], block_v, local_sems.at[4]),
        pltpu.make_async_copy(pat_hbm, pat_ref, local_sems.at[5]),
        pltpu.make_async_copy(ext_hbm, ext_ref, local_sems.at[6]),
    ]
    for load in loads:
        load.start()

    barrier = pltpu.get_barrier_semaphore()
    greeted = [sibling, x_next[1], x_next[-1], x_cross[1], x_cross[-1], x_far, z_next[1], z_next[-1]]
    for other in greeted:
        pl.semaphore_signal(barrier, inc=1, device_id=other, device_id_type=MESH)

    wires = Wires(send_sems, recv_sems, pair_sems, cbuf, sibling)
    def c_at(dx):
        return lambda dz, first, count: c_slot(dx, dz, core, first, count)

    def u_at(dx):
        return lambda dz, first, count: u_slot(dx, dz, core, first, count)

    def g_rows(half, way):
        start = half * 256 + (0 if way == 1 else 128) + core * 64
        return gbuf.at[pl.ds(pl.multiple_of(start, 64), 64)]

    def arrived(name):
        kind = name[0]
        if kind == "g":
            return g_rows(1 - low, name[1])
        if kind == "u":
            if name[1] == "far":
                return u_slot(2, 0, core)
            _, dx, way, step = name
            return u_slot(dx, -way * step, core, *span(0, ROWS, step, way))
        if kind == "a" and name[1] == "z":
            _, _, way, step = name
            return c_slot(0, -way * step, core, *span(0, CUT, step, way))
        if kind == "a":
            _, step, way, reach, side = name
            rows = span(0, CUT, step, way)
            if reach == "x":
                return c_slot(-side, -way * step, core, *rows)
            return c_slot(2, -way * step, core, *part(*rows, side))
        if name[1] == "x":
            return c_slot(-name[2], 0, core, CUT, TAIL)
        if name[1] == "xx":
            return c_slot(2, 0, core, *part(CUT, TAIL, name[2]))
        _, _, way, step = name
        return c_line(-way * step, core, *span(CUT, TAIL, step, way))

    def leaving(name):
        kind = name[0]
        if kind == "g":
            return g_rows(low, name[1]), x_next[name[1]]
        if kind == "u":
            if name[1] == "far":
                return (u_slot(0, 0, core), u_slot(2, 0, core)), x_far
            _, dx, way, step = name
            return u_slot(dx, -way * (step - 1), core, *span(0, ROWS, step, way)), z_next[way]
        if kind == "a" and name[1] == "z":
            _, _, way, step = name
            return c_slot(0, -way * (step - 1), core, *span(0, CUT, step, way)), z_next[way]
        if kind == "a":
            _, step, way, reach, side = name
            rows = span(0, CUT, step, way)
            if reach == "x":
                return c_slot(0, -way * step, core, *rows), x_next[side]
            return c_slot(-side, -way * step, core, *part(*rows, side)), x_next[side]
        if name[1] == "x":
            return c_slot(0, 0, core, CUT, TAIL), x_next[name[2]]
        if name[1] == "xx":
            return c_slot(-name[2], 0, core, *part(CUT, TAIL, name[2])), x_next[name[2]]
        _, _, way, step = name
        return c_line(-way * (step - 1), core, *span(CUT, TAIL, step, way)), z_next[way]

    col_rows = pl.multiple_of(core * 128, 128)

    def cols_near(to_core):
        return wires.copy(
            ubuf.at[0, z % 4, pl.ds(pl.multiple_of(to_core * 128 + core * ROWS, ROWS), ROWS)],
            ucols.at[pl.ds(pl.multiple_of(core * ROWS, ROWS), ROWS)],
            cols_sems.at[0, to_core],
            cols_sems.at[1, core],
            device(across(1), z, to_core),
        )

    def cols_arrive():
        for from_core in range(2):
            piece = ucols.at[pl.ds(from_core * ROWS, ROWS)]
            wires.copy(piece, piece, cols_sems.at[0, 0], cols_sems.at[1, from_core], sibling).wait_recv()

    def own_panel():
        loads[0].wait()
        loads[1].wait()
        loads[5].wait()
        own_tile = grid // 4
        keep = [pat_ref[0, side, own_tile].astype(F32) for side in range(2)]
        masked = jnp.concatenate([panel_v[:, :256] * keep[0], panel_v[:, 256:] * keep[1]], axis=1)
        inv_high, inv_low = split(cinv_v[...])
        cbuf[low, high, z // 2, rows_of(z, core, 0, ROWS), :] = dot3(nt, masked, inv_high, inv_low)

    pl.semaphore_wait(barrier, len(greeted))

    def source(child, parent_tile):
        row = y * 2 + child
        side, line, found = jnp.int32(0), jnp.int32(0), jnp.int32(0)
        for position in range(8):
            hit = ext_ref[row, position] == parent_tile
            side, line = jnp.where(hit, position // 4, side), jnp.where(hit, position % 4, line)
            found = jnp.where(hit, 1, found)
        return side, line, found.astype(F32)

    def inverse():
        wires.pair_arrive(2)
        g_high[...], g_low[...] = split(gbuf[...])

    def pivots():
        wires.pair_arrive(0)
        loads[6].wait()
        for child in range(2):
            side, line, found = source(child, 2 + high * 8 + z)
            fcols[child] = cbuf[child, side, line, pl.ds(col_rows, 128), :] * found
            for pivot in range(2):
                side, line, found = source(child, jnp.int32(pivot))
                p_high[pivot, child], p_low[pivot, child] = split(cbuf[child, side, line] * found)

    def hat():
        wires.pair_arrive(1)
        wires.pair_arrive(3)
        for where, far in ((0, 0), (3, 1)):
            @pl.when(place == where)
            def _(far=far):
                ucols[...] = ubuf[far, z % 4, pl.ds(col_rows, 128), :]

        for pivot in range(2):
            total = ucols[:, pivot * 256 : (pivot + 1) * 256]
            for child in range(2):
                total = total - dot3(nt, fcols[child], p_high[pivot, child], p_low[pivot, child])
            hats[:, pivot * 256 : (pivot + 1) * 256] = total

    def weight():
        weights[...] = dot3(nt, hats[...], g_high[...], g_low[...])

    def back():
        hats[...] = dot3(nn, weights[...], g_high[...], g_low[...])
        y_cat[...] = stack(hats[...])

    def narrow():
        for child in range(2):
            total = fcols[child]
            for pivot in range(2):
                total = total - dot3(
                    nn, hats[:, pivot * 256 : (pivot + 1) * 256], p_high[pivot, child], p_low[pivot, child]
                )
            b_cat[child] = stack(total)
        loads[4].wait()

    def times(value, right):
        value_high, value_low = split(value)
        wide = nt(value_high, right)
        return wide[:, :128] + wide[:, 128:] + nt(value_low, right[:128])

    def tile(index):
        at = (high * 4 + index) % 8
        rows = pl.ds(pl.multiple_of(at * TILE, TILE), TILE)
        total = block_v[rows, :] - times(ubuf[index // 4, index % 4], y_cat[...])
        for child in range(2):
            side, line, found = source(child, 2 + low * 8 + at)
            total = total - times(cbuf[child, side, line], b_cat[child]) * found
        out_ref[0, rows, :] = total

    computing = dict(
        inverse=inverse, pivots=pivots, hat=hat, weight=weight, back=back, narrow=narrow,
        tile=tile,
    )

    held, lines = [], {}

    def release():
        for item in held:
            wires.pair(*item)
        held.clear()

    def pair_kind(name):
        if name[0] == "u":
            return 1 if name[1] == 0 else 3
        return 2 if name[0] == "g" else 0

    for action, name in plan():
        if action == "work":
            release()
            if isinstance(name, tuple):
                computing[name[0]](name[1])
            else:
                computing[name]()
        elif action == "wait":
            release()
            if name == "U":
                loads[2].wait()
                held.append((1, u_slot(0, 0, core)))
            elif name == "G":
                loads[3].wait()
            elif name == "C":
                own_panel()
            elif name == ("cols", "near"):
                pl.when(jnp.logical_or(place == 1, place == 2))(cols_arrive)
            else:
                piece = arrived(name)
                wires.arrive(name, piece)
                if name[0] in "ab" and name[1] != "z":
                    line, rows = (name[1:3], (0, CUT)) if name[0] == "a" else ((0, 1), (CUT, TAIL))
                    lines[line, rows] = lines.get((line, rows), 0) + 1
                    if lines[line, rows] == 4:
                        step, way = line
                        held.append((0, c_line(-way * step, core, *span(*rows, step, way))))
                elif name[:2] != ("a", "z"):
                    held.append((pair_kind(name), piece))
        elif name == ("cols", "near"):
            @pl.when(place < 2)
            def _():
                for to_core in range(2):
                    cols_near(to_core).start()
        else:
            wires.send(name, *leaving(name))

    wires.drain()

    @pl.when(place < 2)
    def _():
        for to_core in range(2):
            cols_near(to_core).wait_send()


def local(panel, pattern, child_inverse, ext_map, upper_rows, parent_inverse, update_block):
    anywhere = pl.BlockSpec(memory_space=pltpu.HBM)
    return pl.pallas_call(
        kernel,
        out_shape=pltpu.VMEM((1, 2048, 128), F32),
        in_specs=[anywhere] * 7,
        out_specs=pl.BlockSpec(memory_space=pltpu.VMEM),
        scratch_shapes=[
            pltpu.VMEM((2, 2, 4, TILE, 512), F32),
            pltpu.VMEM((2, 4, TILE, 512), F32),
            pltpu.VMEM((128, 512), F32),
            pltpu.VMEM((2, 128, 512), F32),
            pltpu.VMEM((128, 512), F32),
            pltpu.VMEM((128, 512), F32),
            pltpu.VMEM((512, 512), F32),
            pltpu.VMEM((ROWS, 512), F32),
            pltpu.VMEM((512, 512), F32),
            pltpu.VMEM((2048, 128), F32),
            pltpu.VMEM((2, 2, TILE, 512), BF16),
            pltpu.VMEM((2, 2, TILE, 512), BF16),
            pltpu.VMEM((512, 512), BF16),
            pltpu.VMEM((512, 512), BF16),
            pltpu.VMEM((2, 256, 512), BF16),
            pltpu.VMEM((256, 512), BF16),
            pltpu.SMEM((8, 8), jnp.int32),
            pltpu.SMEM((1, 2, 8), jnp.int32),
            pltpu.SemaphoreType.DMA((7,)),
            pltpu.SemaphoreType.DMA((2,)),
            pltpu.SemaphoreType.DMA((len(messages()[0]) - 1,)),
            pltpu.SemaphoreType.DMA((4,)),
            pltpu.SemaphoreType.DMA((2, 2)),
        ],
        compiler_params=pltpu.CompilerParams(
            collective_id=0, has_side_effects=True, vmem_limit_bytes=60 * 2**20
        ),
    )(ext_map, jnp.swapaxes(pattern, 1, 2), panel, child_inverse, upper_rows, parent_inverse, update_block)


def solution(mesh):
    in_specs = (
        P("cube", "grid", None),
        P("cube", None, None),
        P("cube", None, None),
        P(),
        P("cube", "grid", None),
        P("cube", None, None),
        P("cube", None, "grid"),
    )
    out_specs = P("cube", None, "grid")
    return jax.shard_map(local, mesh=mesh, in_specs=in_specs, out_specs=out_specs, check_vma=False)
```

```python
import math

import jax
import jax.numpy as jnp
from jax import lax
from jax.experimental import pallas as pl
from jax.experimental.pallas import tpu as pltpu
from jax.sharding import PartitionSpec as P

MESH = pl.DeviceIdType.MESH
F32 = jnp.float32
BF16 = jnp.bfloat16
NX, NZ = 4, 8
ROWS = 64
CUT = 48
TILE = 256


def nt(left, right):
    return lax.dot_general(left, right, (((1,), (1,)), ((), ())), preferred_element_type=F32)


def nn(left, right):
    return lax.dot_general(left, right, (((1,), (0,)), ((), ())), preferred_element_type=F32)


def split(value):
    high = value.astype(BF16)
    return high, (value - high.astype(F32)).astype(BF16)


def stack(value):
    return jnp.concatenate(split(value), axis=0)


def dot3(mul, left, right_high, right_low):
    count = left.shape[0]
    both = stack(left)
    wide = mul(both, right_high)
    return wide[:count] + wide[count:] + mul(both[:count], right_low)


WAYS = (1, -1)
LAST = NZ // 2
TAIL = ROWS - CUT
ROW_TIME, LATENCY, AHEAD, STEP, READY = 0.043, 2.3, 2.4, 0.08, 1.5
PAIR = 1.0
WEIGHT = {("b", "z"): -4.0, ("a", "z"): 3.0}


def span(first, count, step, way):
    if step < LAST:
        return first, count
    return (first, count // 2) if way == 1 else (first + count // 2, count // 2)


def part(first, count, side):
    front = max(count // 24, 1) * 8
    return (first, front) if side == 1 else (first + front, count - front)


def messages():
    table, after = {}, {}

    def add(name, links, count, *needs):
        table[name], after[name] = (links, count), needs

    def ring(base, needs, first, count, times=1):
        for way in WAYS:
            before = needs
            for step in range(1, LAST + 1):
                add(base + (way, step), (("z", way),), span(first, count, step, way)[1] * times, *before)
                before = (base + (way, step),)

    ring(("a", "z"), ("C",), 0, CUT)
    for step in range(LAST + 1):
        for way in WAYS if step else (1,):
            first, count = span(0, CUT, step, way)
            for side in WAYS:
                near = ("a", step, way, "x", side)
                add(near, (("x", side),), count, ("a", "z", way, step) if step else "C")
                add(near[:3] + ("xx", side), (("x", side),), part(first, count, side)[1], near)
    for side in WAYS:
        add(("b", "x", side), (("x", side),), TAIL, "C")
        add(("b", "xx", side), (("x", side),), part(CUT, TAIL, side)[1], ("b", "x", side))
    joined = tuple(("b", reach, side) for reach in ("x", "xx") for side in WAYS)
    ring(("b", "z"), joined, CUT, TAIL, NX)
    ring(("u", 0), ("U",), 0, ROWS)
    add(("u", "far"), (("x", 1), ("x", -1)), ROWS, "U")
    ring(("u", 2), (("u", "far"),), 0, ROWS)
    near_u = tuple(name for name in table if name[:2] == ("u", 0))
    for side in WAYS:
        add(("g", side), (("x", side),), ROWS, "G")
    add(("cols", "near"), (("x", 1),), 2 * ROWS, *near_u)
    return table, after


def work(table):
    def of(*kinds):
        return [name for name in table if name[0] in kinds]

    tasks = [("inverse", of("g"), 0.3), ("pivots", of("a", "b"), 0.5), ("hat", of("cols", "u"), 0.6)]
    tasks += [("weight", (), 0.5), ("back", (), 0.5), ("narrow", (), 0.5)]
    return tasks + [(("tile", index), (), 0.45) for index in range(8)]


def plan():
    table, after = messages()
    tasks, landed = work(table), {}
    users = {}
    for name, needs in after.items():
        for need in needs:
            users.setdefault(need, []).append(name)
    chain = {}

    def length(name):
        if name not in chain:
            chain[name] = max(
                (length(user) + LATENCY + table[user][1] * ROW_TIME for user in users.get(name, ())), default=0.0
            )
        return chain[name]

    def rank(name):
        return length(name) + WEIGHT.get(name[:2], 0.0)

    links = [(axis, way) for axis in "xz" for way in WAYS]
    free = {link: 0.0 for link in links}
    ready = []
    missing = {name: len(needs) for name, needs in after.items()}
    now, events, order = 0.0, [(0.0, 0, "U"), (0.1, 1, "G"), (READY, 2, "C")], []
    number = 3
    while events or tasks:
        events.sort()
        if tasks and all(need in landed for need in tasks[0][1]):
            start = max([0.0] + [landed[need] + PAIR for need in tasks[0][1]])
            if not events or max(start, now) < events[0][0]:
                now = max(start, now) + tasks[0][2]
                order.append(("work", tasks.pop(0)[0]))
                continue
        time, _, name = events.pop(0)
        now = max(now, time) + 2 * STEP
        landed[name] = now
        order.append(("wait", name))
        for user in users.get(name, ()):
            missing[user] -= 1
            if not missing[user]:
                ready.append(user)
        ready.sort(key=lambda user: -rank(user))
        for user in list(ready):
            over, count = table[user]
            if max(free[link] for link in over) - now > AHEAD:
                continue
            ready.remove(user)
            end = max([now] + [free[link] for link in over]) + count * ROW_TIME
            for link in over:
                free[link] = end
            events.append((end + LATENCY, number, user))
            number += 1
            order.append(("send", user))
            now += STEP
    assert not ready
    return order


def rows_in(piece):
    return math.prod(piece.shape[:-1])


class Wires:
    def __init__(self, send_sems, recv_sems, pair_sems, model, any_device):
        self.send_sems, self.recv_sems, self.pair_sems = send_sems, recv_sems, pair_sems
        self.model, self.any_device = model, any_device
        self.number, self.sent, self.paired = {}, {}, {}

    def copy(self, source, target, send_sem, recv_sem, device):
        return pltpu.make_async_remote_copy(
            src_ref=source,
            dst_ref=target,
            send_sem=send_sem,
            recv_sem=recv_sem,
            device_id=device,
            device_id_type=MESH,
        )

    def named(self, name):
        return self.recv_sems.at[self.number.setdefault(name, len(self.number))]

    def send(self, name, piece, device):
        piece, target = piece if isinstance(piece, tuple) else (piece, piece)
        self.copy(piece, target, self.send_sems.at[0], self.named(name), device).start()
        self.sent[0] = self.sent.get(0, 0) + rows_in(piece)

    def arrive(self, name, piece):
        self.copy(piece, piece, self.send_sems.at[0], self.named(name), self.any_device).wait_recv()

    def pair(self, kind, piece):
        self.copy(piece, piece, self.send_sems.at[1], self.pair_sems.at[kind], self.any_device).start()
        self.sent[1] = self.sent.get(1, 0) + rows_in(piece)
        self.paired[kind] = self.paired.get(kind, 0) + rows_in(piece)

    def rows(self, count):
        for tiles in (16, 8, 4, 3, 2, 1):
            if count % (8 * tiles) == 0 and count // tiles <= TILE:
                both, half, line = 2 if tiles > 8 else 1, 2 if tiles > 4 else 1, min(tiles, 4)
                return self.model.at[pl.ds(0, both), pl.ds(0, half), pl.ds(0, line), pl.ds(0, count // tiles)]
        raise ValueError(count)

    def pair_arrive(self, kind):
        piece = self.rows(self.paired[kind])
        self.copy(piece, piece, self.send_sems.at[1], self.pair_sems.at[kind], self.any_device).wait_recv()

    def drain(self):
        for kind, count in self.sent.items():
            piece = self.rows(count)
            self.copy(piece, piece, self.send_sems.at[kind], self.pair_sems.at[0], self.any_device).wait_send()


def kernel(
    ext_hbm, pat_hbm, panel_ref, cinv_ref, upper_ref, pinv_ref, block_ref, out_ref,
    cbuf, ubuf, ucols, fcols, hats, weights, gbuf, panel_v, cinv_v, block_v,
    p_high, p_low, g_high, g_low, b_cat, y_cat, ext_ref, pat_ref,
    local_sems, send_sems, recv_sems, pair_sems, cols_sems,
):
    cube, grid = lax.axis_index("cube"), lax.axis_index("grid")
    y, low = cube // 2, cube % 2
    high, z, core = grid // 16, (grid % 16) // 2, grid % 2
    x = high * 2 + low

    def device(xx, zz, cc):
        return (y * 2 + xx % 2, (xx // 2) * 16 + zz * 2 + cc)

    turn = jnp.where(z < NZ // 2, 1, -1)
    place = jnp.where(z < NZ // 2, x, NX - 1 - x)

    def across(dx):
        return (x + dx * turn + NX) % NX

    sibling = device(x, z, 1 - core)
    x_next = {1: device(across(1), z, core), -1: device(across(-1), z, core)}
    x_cross = {1: device(across(1), z, 1 - core), -1: device(across(-1), z, 1 - core)}
    x_far = device((x + 2) % NX, z, core)
    z_next = {1: device(x, (z + 1) % NZ, core), -1: device(x, (z + 7) % NZ, core)}

    def rows_of(zz, cc, first, count):
        return pl.ds(pl.multiple_of((zz % 2) * 128 + cc * ROWS + first, 8), count)

    def c_slot(dx, dz, cc, first=0, count=ROWS):
        xx, zz = across(dx), (z + dz + NZ) % NZ
        return cbuf.at[xx % 2, xx // 2, zz // 2, rows_of(zz, cc, first, count)]

    def c_line(dz, cc, first, count):
        zz = (z + dz + NZ) % NZ
        return cbuf.at[:, :, zz // 2, rows_of(zz, cc, first, count)]

    def u_slot(far, dz, cc, first=0, count=ROWS):
        zz = (z + dz + NZ) % NZ
        return ubuf.at[1 if far else 0, zz // 2, rows_of(zz, cc, first, count)]

    loads = [
        pltpu.make_async_copy(panel_ref.at[0], panel_v, local_sems.at[0]),
        pltpu.make_async_copy(cinv_ref.at[0], cinv_v, local_sems.at[1]),
        pltpu.make_async_copy(upper_ref.at[0], u_slot(0, 0, core), local_sems.at[2]),
        pltpu.make_async_copy(
            pinv_ref.at[0], gbuf.at[pl.ds(pl.multiple_of(low * 256, 256), 256)], local_sems.at[3]
        ),
        pltpu.make_async_copy(block_ref.at[0], block_v, local_sems.at[4]),
        pltpu.make_async_copy(pat_hbm, pat_ref, local_sems.at[5]),
        pltpu.make_async_copy(ext_hbm, ext_ref, local_sems.at[6]),
    ]
    for load in loads:
        load.start()

    barrier = pltpu.get_barrier_semaphore()
    greeted = [sibling, x_next[1], x_next[-1], x_cross[1], x_cross[-1], x_far, z_next[1], z_next[-1]]
    for other in greeted:
        pl.semaphore_signal(barrier, inc=1, device_id=other, device_id_type=MESH)

    wires = Wires(send_sems, recv_sems, pair_sems, cbuf, sibling)
    def c_at(dx):
        return lambda dz, first, count: c_slot(dx, dz, core, first, count)

    def u_at(dx):
        return lambda dz, first, count: u_slot(dx, dz, core, first, count)

    def g_rows(half, way):
        start = half * 256 + (0 if way == 1 else 128) + core * 64
        return gbuf.at[pl.ds(pl.multiple_of(start, 64), 64)]

    def arrived(name):
        kind = name[0]
        if kind == "g":
            return g_rows(1 - low, name[1])
        if kind == "u":
            if name[1] == "far":
                return u_slot(2, 0, core)
            _, dx, way, step = name
            return u_slot(dx, -way * step, core, *span(0, ROWS, step, way))
        if kind == "a" and name[1] == "z":
            _, _, way, step = name
            return c_slot(0, -way * step, core, *span(0, CUT, step, way))
        if kind == "a":
            _, step, way, reach, side = name
            rows = span(0, CUT, step, way)
            if reach == "x":
                return c_slot(-side, -way * step, core, *rows)
            return c_slot(2, -way * step, core, *part(*rows, side))
        if name[1] == "x":
            return c_slot(-name[2], 0, core, CUT, TAIL)
        if name[1] == "xx":
            return c_slot(2, 0, core, *part(CUT, TAIL, name[2]))
        _, _, way, step = name
        return c_line(-way * step, core, *span(CUT, TAIL, step, way))

    def leaving(name):
        kind = name[0]
        if kind == "g":
            return g_rows(low, name[1]), x_next[name[1]]
        if kind == "u":
            if name[1] == "far":
                return (u_slot(0, 0, core), u_slot(2, 0, core)), x_far
            _, dx, way, step = name
            return u_slot(dx, -way * (step - 1), core, *span(0, ROWS, step, way)), z_next[way]
        if kind == "a" and name[1] == "z":
            _, _, way, step = name
            return c_slot(0, -way * (step - 1), core, *span(0, CUT, step, way)), z_next[way]
        if kind == "a":
            _, step, way, reach, side = name
            rows = span(0, CUT, step, way)
            if reach == "x":
                return c_slot(0, -way * step, core, *rows), x_next[side]
            return c_slot(-side, -way * step, core, *part(*rows, side)), x_next[side]
        if name[1] == "x":
            return c_slot(0, 0, core, CUT, TAIL), x_next[name[2]]
        if name[1] == "xx":
            return c_slot(-name[2], 0, core, *part(CUT, TAIL, name[2])), x_next[name[2]]
        _, _, way, step = name
        return c_line(-way * (step - 1), core, *span(CUT, TAIL, step, way)), z_next[way]

    col_rows = pl.multiple_of(core * 128, 128)

    def cols_near(to_core):
        return wires.copy(
            ubuf.at[0, z % 4, pl.ds(pl.multiple_of(to_core * 128 + core * ROWS, ROWS), ROWS)],
            ucols.at[pl.ds(pl.multiple_of(core * ROWS, ROWS), ROWS)],
            cols_sems.at[0, to_core],
            cols_sems.at[1, core],
            device(across(1), z, to_core),
        )

    def cols_arrive():
        for from_core in range(2):
            piece = ucols.at[pl.ds(from_core * ROWS, ROWS)]
            wires.copy(piece, piece, cols_sems.at[0, 0], cols_sems.at[1, from_core], sibling).wait_recv()

    def own_panel():
        loads[0].wait()
        loads[1].wait()
        loads[5].wait()
        own_tile = grid // 4
        keep = [pat_ref[0, side, own_tile].astype(F32) for side in range(2)]
        masked = jnp.concatenate([panel_v[:, :256] * keep[0], panel_v[:, 256:] * keep[1]], axis=1)
        inv_high, inv_low = split(cinv_v[...])
        cbuf[low, high, z // 2, rows_of(z, core, 0, ROWS), :] = dot3(nt, masked, inv_high, inv_low)

    pl.semaphore_wait(barrier, len(greeted))

    def source(child, parent_tile):
        row = y * 2 + child
        side, line, found = jnp.int32(0), jnp.int32(0), jnp.int32(0)
        for position in range(8):
            hit = ext_ref[row, position] == parent_tile
            side, line = jnp.where(hit, position // 4, side), jnp.where(hit, position % 4, line)
            found = jnp.where(hit, 1, found)
        return side, line, found.astype(F32)

    def inverse():
        wires.pair_arrive(2)
        g_high[...], g_low[...] = split(gbuf[...])

    def pivots():
        wires.pair_arrive(0)
        loads[6].wait()
        for child in range(2):
            side, line, found = source(child, 2 + high * 8 + z)
            fcols[child] = cbuf[child, side, line, pl.ds(col_rows, 128), :] * found
            for pivot in range(2):
                side, line, found = source(child, jnp.int32(pivot))
                p_high[pivot, child], p_low[pivot, child] = split(cbuf[child, side, line] * found)

    def hat():
        wires.pair_arrive(1)
        wires.pair_arrive(3)
        for where, far in ((0, 0), (3, 1)):
            @pl.when(place == where)
            def _(far=far):
                ucols[...] = ubuf[far, z % 4, pl.ds(col_rows, 128), :]

        for pivot in range(2):
            total = ucols[:, pivot * 256 : (pivot + 1) * 256]
            for child in range(2):
                total = total - dot3(nt, fcols[child], p_high[pivot, child], p_low[pivot, child])
            hats[:, pivot * 256 : (pivot + 1) * 256] = total

    def weight():
        weights[...] = dot3(nt, hats[...], g_high[...], g_low[...])

    def back():
        hats[...] = dot3(nn, weights[...], g_high[...], g_low[...])
        y_cat[...] = stack(hats[...])

    def narrow():
        for child in range(2):
            total = fcols[child]
            for pivot in range(2):
                total = total - dot3(
                    nn, hats[:, pivot * 256 : (pivot + 1) * 256], p_high[pivot, child], p_low[pivot, child]
                )
            b_cat[child] = stack(total)
        loads[4].wait()

    def times(value, right):
        value_high, value_low = split(value)
        wide = nt(value_high, right)
        return wide[:, :128] + wide[:, 128:] + nt(value_low, right[:128])

    def tile(index):
        at = (high * 4 + index) % 8
        rows = pl.ds(pl.multiple_of(at * TILE, TILE), TILE)
        total = block_v[rows, :] - times(ubuf[index // 4, index % 4], y_cat[...])
        for child in range(2):
            side, line, found = source(child, 2 + low * 8 + at)
            total = total - times(cbuf[child, side, line], b_cat[child]) * found
        out_ref[0, rows, :] = total

    computing = dict(
        inverse=inverse, pivots=pivots, hat=hat, weight=weight, back=back, narrow=narrow,
        tile=tile,
    )

    held, lines = [], {}

    def release():
        for item in held:
            wires.pair(*item)
        held.clear()

    def pair_kind(name):
        if name[0] == "u":
            return 1 if name[1] == 0 else 3
        return 2 if name[0] == "g" else 0

    for action, name in plan():
        if action == "work":
            release()
            if isinstance(name, tuple):
                computing[name[0]](name[1])
            else:
                computing[name]()
        elif action == "wait":
            release()
            if name == "U":
                loads[2].wait()
                held.append((1, u_slot(0, 0, core)))
            elif name == "G":
                loads[3].wait()
            elif name == "C":
                own_panel()
            elif name == ("cols", "near"):
                pl.when(jnp.logical_or(place == 1, place == 2))(cols_arrive)
            else:
                piece = arrived(name)
                wires.arrive(name, piece)
                if name[0] == "a" and LAST in name[1:4]:
                    held.append((0, piece))
                elif name[0] in "ab" and name[1] != "z":
                    line, rows = (name[1:3], (0, CUT)) if name[0] == "a" else ((0, 1), (CUT, TAIL))
                    lines[line, rows] = lines.get((line, rows), 0) + 1
                    if lines[line, rows] == 4:
                        step, way = line
                        held.append((0, c_line(-way * step, core, *span(*rows, step, way))))
                elif name[:2] != ("a", "z"):
                    held.append((pair_kind(name), piece))
        elif name == ("cols", "near"):
            @pl.when(place < 2)
            def _():
                for to_core in range(2):
                    cols_near(to_core).start()
        else:
            wires.send(name, *leaving(name))

    wires.drain()

    @pl.when(place < 2)
    def _():
        for to_core in range(2):
            cols_near(to_core).wait_send()


def local(panel, pattern, child_inverse, ext_map, upper_rows, parent_inverse, update_block):
    anywhere = pl.BlockSpec(memory_space=pltpu.HBM)
    return pl.pallas_call(
        kernel,
        out_shape=pltpu.VMEM((1, 2048, 128), F32),
        in_specs=[anywhere] * 7,
        out_specs=pl.BlockSpec(memory_space=pltpu.VMEM),
        scratch_shapes=[
            pltpu.VMEM((2, 2, 4, TILE, 512), F32),
            pltpu.VMEM((2, 4, TILE, 512), F32),
            pltpu.VMEM((128, 512), F32),
            pltpu.VMEM((2, 128, 512), F32),
            pltpu.VMEM((128, 512), F32),
            pltpu.VMEM((128, 512), F32),
            pltpu.VMEM((512, 512), F32),
            pltpu.VMEM((ROWS, 512), F32),
            pltpu.VMEM((512, 512), F32),
            pltpu.VMEM((2048, 128), F32),
            pltpu.VMEM((2, 2, TILE, 512), BF16),
            pltpu.VMEM((2, 2, TILE, 512), BF16),
            pltpu.VMEM((512, 512), BF16),
            pltpu.VMEM((512, 512), BF16),
            pltpu.VMEM((2, 256, 512), BF16),
            pltpu.VMEM((256, 512), BF16),
            pltpu.SMEM((8, 8), jnp.int32),
            pltpu.SMEM((1, 2, 8), jnp.int32),
            pltpu.SemaphoreType.DMA((7,)),
            pltpu.SemaphoreType.DMA((2,)),
            pltpu.SemaphoreType.DMA((len(messages()[0]) - 1,)),
            pltpu.SemaphoreType.DMA((4,)),
            pltpu.SemaphoreType.DMA((2, 2)),
        ],
        compiler_params=pltpu.CompilerParams(
            collective_id=0, has_side_effects=True, vmem_limit_bytes=60 * 2**20
        ),
    )(ext_map, jnp.swapaxes(pattern, 1, 2), panel, child_inverse, upper_rows, parent_inverse, update_block)


def solution(mesh):
    in_specs = (
        P("cube", "grid", None),
        P("cube", None, None),
        P("cube", None, None),
        P(),
        P("cube", "grid", None),
        P("cube", None, None),
        P("cube", None, "grid"),
    )
    out_specs = P("cube", None, "grid")
    return jax.shard_map(local, mesh=mesh, in_specs=in_specs, out_specs=out_specs, check_vma=False)
```

```python
import math

import jax
import jax.numpy as jnp
from jax import lax
from jax.experimental import pallas as pl
from jax.experimental.pallas import tpu as pltpu
from jax.sharding import PartitionSpec as P

MESH = pl.DeviceIdType.MESH
F32 = jnp.float32
BF16 = jnp.bfloat16
NX, NZ = 4, 8
ROWS = 64
CUT = 48
TILE = 256


def nt(left, right):
    return lax.dot_general(left, right, (((1,), (1,)), ((), ())), preferred_element_type=F32)


def nn(left, right):
    return lax.dot_general(left, right, (((1,), (0,)), ((), ())), preferred_element_type=F32)


def split(value):
    high = value.astype(BF16)
    return high, (value - high.astype(F32)).astype(BF16)


def stack(value):
    return jnp.concatenate(split(value), axis=0)


def dot3(mul, left, right_high, right_low):
    count = left.shape[0]
    both = stack(left)
    wide = mul(both, right_high)
    return wide[:count] + wide[count:] + mul(both[:count], right_low)


WAYS = (1, -1)
LAST = NZ // 2
TAIL = ROWS - CUT
ROW_TIME, LATENCY, AHEAD, STEP, READY = 0.043, 2.3, 2.4, 0.08, 1.5
PAIR = 1.0
WEIGHT = {("b", "z"): -4.0, ("a", "z"): 3.0}


def span(first, count, step, way):
    if step < LAST:
        return first, count
    return (first, count // 2) if way == 1 else (first + count // 2, count // 2)


def part(first, count, side):
    front = max(count // 24, 1) * 8
    return (first, front) if side == 1 else (first + front, count - front)


def messages():
    table, after = {}, {}

    def add(name, links, count, *needs):
        table[name], after[name] = (links, count), needs

    def ring(base, needs, first, count, times=1):
        for way in WAYS:
            before = needs
            for step in range(1, LAST + 1):
                add(base + (way, step), (("z", way),), span(first, count, step, way)[1] * times, *before)
                before = (base + (way, step),)

    ring(("a", "z"), ("C",), 0, CUT)
    for step in range(LAST + 1):
        for way in WAYS if step else (1,):
            first, count = span(0, CUT, step, way)
            for side in WAYS:
                near = ("a", step, way, "x", side)
                add(near, (("x", side),), count, ("a", "z", way, step) if step else "C")
                add(near[:3] + ("xx", side), (("x", side),), part(first, count, side)[1], near)
    for side in WAYS:
        add(("b", "x", side), (("x", side),), TAIL, "C")
        add(("b", "xx", side), (("x", side),), part(CUT, TAIL, side)[1], ("b", "x", side))
    joined = tuple(("b", reach, side) for reach in ("x", "xx") for side in WAYS)
    ring(("b", "z"), joined, CUT, TAIL, NX)
    ring(("u", 0), ("U",), 0, ROWS)
    add(("u", "far"), (("x", 1), ("x", -1)), ROWS, "U")
    ring(("u", 2), (("u", "far"),), 0, ROWS)
    near_u = tuple(name for name in table if name[:2] == ("u", 0))
    for side in WAYS:
        add(("g", side), (("x", side),), ROWS, "G")
    add(("cols", "near"), (("x", 1),), 2 * ROWS, *near_u)
    return table, after


def work(table):
    def of(*kinds):
        return [name for name in table if name[0] in kinds]

    tasks = [("inverse", of("g"), 0.3), ("pivots", of("a", "b"), 0.5), ("hat", of("cols", "u"), 0.6)]
    tasks += [("weight", (), 0.5), ("back", (), 0.5), ("narrow", (), 0.5)]
    return tasks + [(("tile", index), (), 0.45) for index in range(8)]


def plan():
    table, after = messages()
    tasks, landed = work(table), {}
    users = {}
    for name, needs in after.items():
        for need in needs:
            users.setdefault(need, []).append(name)
    chain = {}

    def length(name):
        if name not in chain:
            chain[name] = max(
                (length(user) + LATENCY + table[user][1] * ROW_TIME for user in users.get(name, ())), default=0.0
            )
        return chain[name]

    def rank(name):
        return length(name) + WEIGHT.get(name[:2], 0.0)

    links = [(axis, way) for axis in "xz" for way in WAYS]
    free = {link: 0.0 for link in links}
    ready = []
    missing = {name: len(needs) for name, needs in after.items()}
    now, events, order = 0.0, [(0.0, 0, "U"), (0.1, 1, "G"), (READY, 2, "C")], []
    number = 3
    while events or tasks:
        events.sort()
        if tasks and all(need in landed for need in tasks[0][1]):
            start = max([0.0] + [landed[need] + PAIR for need in tasks[0][1]])
            if not events or max(start, now) < events[0][0]:
                now = max(start, now) + tasks[0][2]
                order.append(("work", tasks.pop(0)[0]))
                continue
        time, _, name = events.pop(0)
        now = max(now, time) + 2 * STEP
        landed[name] = now
        order.append(("wait", name))
        for user in users.get(name, ()):
            missing[user] -= 1
            if not missing[user]:
                ready.append(user)
        ready.sort(key=lambda user: -rank(user))
        for user in list(ready):
            over, count = table[user]
            if max(free[link] for link in over) - now > AHEAD:
                continue
            ready.remove(user)
            end = max([now] + [free[link] for link in over]) + count * ROW_TIME
            for link in over:
                free[link] = end
            events.append((end + LATENCY, number, user))
            number += 1
            order.append(("send", user))
            now += STEP
    assert not ready
    return order


def rows_in(piece):
    return math.prod(piece.shape[:-1])


class Wires:
    def __init__(self, send_sems, recv_sems, pair_sems, model, any_device):
        self.send_sems, self.recv_sems, self.pair_sems = send_sems, recv_sems, pair_sems
        self.model, self.any_device = model, any_device
        self.number, self.sent, self.paired = {}, {}, {}

    def copy(self, source, target, send_sem, recv_sem, device):
        return pltpu.make_async_remote_copy(
            src_ref=source,
            dst_ref=target,
            send_sem=send_sem,
            recv_sem=recv_sem,
            device_id=device,
            device_id_type=MESH,
        )

    def named(self, name):
        name = name[:-1] if "xx" in name else name
        return self.recv_sems.at[self.number.setdefault(name, len(self.number))]

    def send(self, name, piece, device):
        piece, target = piece if isinstance(piece, tuple) else (piece, piece)
        self.copy(piece, target, self.send_sems.at[0], self.named(name), device).start()
        self.sent[0] = self.sent.get(0, 0) + rows_in(piece)

    def arrive(self, name, piece):
        self.copy(piece, piece, self.send_sems.at[0], self.named(name), self.any_device).wait_recv()

    def pair(self, kind, piece):
        self.copy(piece, piece, self.send_sems.at[1], self.pair_sems.at[kind], self.any_device).start()
        self.sent[1] = self.sent.get(1, 0) + rows_in(piece)
        self.paired[kind] = self.paired.get(kind, 0) + rows_in(piece)

    def rows(self, count):
        for tiles in (16, 8, 4, 3, 2, 1):
            if count % (8 * tiles) == 0 and count // tiles <= TILE:
                both, half, line = 2 if tiles > 8 else 1, 2 if tiles > 4 else 1, min(tiles, 4)
                return self.model.at[pl.ds(0, both), pl.ds(0, half), pl.ds(0, line), pl.ds(0, count // tiles)]
        raise ValueError(count)

    def pair_arrive(self, kind):
        piece = self.rows(self.paired[kind])
        self.copy(piece, piece, self.send_sems.at[1], self.pair_sems.at[kind], self.any_device).wait_recv()

    def drain(self):
        for kind, count in self.sent.items():
            piece = self.rows(count)
            self.copy(piece, piece, self.send_sems.at[kind], self.pair_sems.at[0], self.any_device).wait_send()


def kernel(
    ext_hbm, pat_hbm, panel_ref, cinv_ref, upper_ref, pinv_ref, block_ref, out_ref,
    cbuf, ubuf, ucols, fcols, hats, weights, gbuf, panel_v, cinv_v, block_v,
    p_high, p_low, g_high, g_low, b_cat, y_cat, ext_ref, pat_ref,
    local_sems, send_sems, recv_sems, pair_sems, cols_sems,
):
    cube, grid = lax.axis_index("cube"), lax.axis_index("grid")
    y, low = cube // 2, cube % 2
    high, z, core = grid // 16, (grid % 16) // 2, grid % 2
    x = high * 2 + low

    def device(xx, zz, cc):
        return (y * 2 + xx % 2, (xx // 2) * 16 + zz * 2 + cc)

    turn = jnp.where(z < NZ // 2, 1, -1)
    place = jnp.where(z < NZ // 2, x, NX - 1 - x)

    def across(dx):
        return (x + dx * turn + NX) % NX

    sibling = device(x, z, 1 - core)
    x_next = {1: device(across(1), z, core), -1: device(across(-1), z, core)}
    x_cross = {1: device(across(1), z, 1 - core), -1: device(across(-1), z, 1 - core)}
    x_far = device((x + 2) % NX, z, core)
    z_next = {1: device(x, (z + 1) % NZ, core), -1: device(x, (z + 7) % NZ, core)}

    def rows_of(zz, cc, first, count):
        return pl.ds(pl.multiple_of((zz % 2) * 128 + cc * ROWS + first, 8), count)

    def c_slot(dx, dz, cc, first=0, count=ROWS):
        xx, zz = across(dx), (z + dz + NZ) % NZ
        return cbuf.at[xx % 2, xx // 2, zz // 2, rows_of(zz, cc, first, count)]

    def c_line(dz, cc, first, count):
        zz = (z + dz + NZ) % NZ
        return cbuf.at[:, :, zz // 2, rows_of(zz, cc, first, count)]

    def u_slot(far, dz, cc, first=0, count=ROWS):
        zz = (z + dz + NZ) % NZ
        return ubuf.at[1 if far else 0, zz // 2, rows_of(zz, cc, first, count)]

    loads = [
        pltpu.make_async_copy(panel_ref.at[0], panel_v, local_sems.at[0]),
        pltpu.make_async_copy(cinv_ref.at[0], cinv_v, local_sems.at[1]),
        pltpu.make_async_copy(upper_ref.at[0], u_slot(0, 0, core), local_sems.at[2]),
        pltpu.make_async_copy(
            pinv_ref.at[0], gbuf.at[pl.ds(pl.multiple_of(low * 256, 256), 256)], local_sems.at[3]
        ),
        pltpu.make_async_copy(block_ref.at[0], block_v, local_sems.at[4]),
        pltpu.make_async_copy(pat_hbm, pat_ref, local_sems.at[5]),
        pltpu.make_async_copy(ext_hbm, ext_ref, local_sems.at[6]),
    ]
    for load in loads:
        load.start()

    barrier = pltpu.get_barrier_semaphore()
    greeted = [sibling, x_next[1], x_next[-1], x_cross[1], x_cross[-1], x_far, z_next[1], z_next[-1]]
    for other in greeted:
        pl.semaphore_signal(barrier, inc=1, device_id=other, device_id_type=MESH)

    wires = Wires(send_sems, recv_sems, pair_sems, cbuf, sibling)
    def c_at(dx):
        return lambda dz, first, count: c_slot(dx, dz, core, first, count)

    def u_at(dx):
        return lambda dz, first, count: u_slot(dx, dz, core, first, count)

    def g_rows(half, way):
        start = half * 256 + (0 if way == 1 else 128) + core * 64
        return gbuf.at[pl.ds(pl.multiple_of(start, 64), 64)]

    def arrived(name):
        kind = name[0]
        if kind == "g":
            return g_rows(1 - low, name[1])
        if kind == "u":
            if name[1] == "far":
                return u_slot(2, 0, core)
            _, dx, way, step = name
            return u_slot(dx, -way * step, core, *span(0, ROWS, step, way))
        if kind == "a" and name[1] == "z":
            _, _, way, step = name
            return c_slot(0, -way * step, core, *span(0, CUT, step, way))
        if kind == "a":
            _, step, way, reach, side = name
            rows = span(0, CUT, step, way)
            if reach == "x":
                return c_slot(-side, -way * step, core, *rows)
            return c_slot(2, -way * step, core, *part(*rows, side))
        if name[1] == "x":
            return c_slot(-name[2], 0, core, CUT, TAIL)
        if name[1] == "xx":
            return c_slot(2, 0, core, *part(CUT, TAIL, name[2]))
        _, _, way, step = name
        return c_line(-way * step, core, *span(CUT, TAIL, step, way))

    def leaving(name):
        kind = name[0]
        if kind == "g":
            return g_rows(low, name[1]), x_next[name[1]]
        if kind == "u":
            if name[1] == "far":
                return (u_slot(0, 0, core), u_slot(2, 0, core)), x_far
            _, dx, way, step = name
            return u_slot(dx, -way * (step - 1), core, *span(0, ROWS, step, way)), z_next[way]
        if kind == "a" and name[1] == "z":
            _, _, way, step = name
            return c_slot(0, -way * (step - 1), core, *span(0, CUT, step, way)), z_next[way]
        if kind == "a":
            _, step, way, reach, side = name
            rows = span(0, CUT, step, way)
            if reach == "x":
                return c_slot(0, -way * step, core, *rows), x_next[side]
            return c_slot(-side, -way * step, core, *part(*rows, side)), x_next[side]
        if name[1] == "x":
            return c_slot(0, 0, core, CUT, TAIL), x_next[name[2]]
        if name[1] == "xx":
            return c_slot(-name[2], 0, core, *part(CUT, TAIL, name[2])), x_next[name[2]]
        _, _, way, step = name
        return c_line(-way * (step - 1), core, *span(CUT, TAIL, step, way)), z_next[way]

    col_rows = pl.multiple_of(core * 128, 128)

    def cols_near(to_core):
        return wires.copy(
            ubuf.at[0, z % 4, pl.ds(pl.multiple_of(to_core * 128 + core * ROWS, ROWS), ROWS)],
            ucols.at[pl.ds(pl.multiple_of(core * ROWS, ROWS), ROWS)],
            cols_sems.at[0, to_core],
            cols_sems.at[1, core],
            device(across(1), z, to_core),
        )

    def cols_arrive():
        for from_core in range(2):
            piece = ucols.at[pl.ds(from_core * ROWS, ROWS)]
            wires.copy(piece, piece, cols_sems.at[0, 0], cols_sems.at[1, from_core], sibling).wait_recv()

    def own_panel():
        loads[0].wait()
        loads[1].wait()
        loads[5].wait()
        own_tile = grid // 4
        keep = [pat_ref[0, side, own_tile].astype(F32) for side in range(2)]
        masked = jnp.concatenate([panel_v[:, :256] * keep[0], panel_v[:, 256:] * keep[1]], axis=1)
        inv_high, inv_low = split(cinv_v[...])
        cbuf[low, high, z // 2, rows_of(z, core, 0, ROWS), :] = dot3(nt, masked, inv_high, inv_low)

    pl.semaphore_wait(barrier, len(greeted))

    def source(child, parent_tile):
        row = y * 2 + child
        side, line, found = jnp.int32(0), jnp.int32(0), jnp.int32(0)
        for position in range(8):
            hit = ext_ref[row, position] == parent_tile
            side, line = jnp.where(hit, position // 4, side), jnp.where(hit, position % 4, line)
            found = jnp.where(hit, 1, found)
        return side, line, found.astype(F32)

    def inverse():
        wires.pair_arrive(2)
        g_high[...], g_low[...] = split(gbuf[...])

    def pivots():
        wires.pair_arrive(0)
        loads[6].wait()
        for child in range(2):
            side, line, found = source(child, 2 + high * 8 + z)
            fcols[child] = cbuf[child, side, line, pl.ds(col_rows, 128), :] * found
            for pivot in range(2):
                side, line, found = source(child, jnp.int32(pivot))
                p_high[pivot, child], p_low[pivot, child] = split(cbuf[child, side, line] * found)

    def hat():
        wires.pair_arrive(1)
        wires.pair_arrive(3)
        for where, far in ((0, 0), (3, 1)):
            @pl.when(place == where)
            def _(far=far):
                ucols[...] = ubuf[far, z % 4, pl.ds(col_rows, 128), :]

        for pivot in range(2):
            total = ucols[:, pivot * 256 : (pivot + 1) * 256]
            for child in range(2):
                total = total - dot3(nt, fcols[child], p_high[pivot, child], p_low[pivot, child])
            hats[:, pivot * 256 : (pivot + 1) * 256] = total

    def weight():
        weights[...] = dot3(nt, hats[...], g_high[...], g_low[...])

    def back():
        hats[...] = dot3(nn, weights[...], g_high[...], g_low[...])
        y_cat[...] = stack(hats[...])

    def narrow():
        for child in range(2):
            total = fcols[child]
            for pivot in range(2):
                total = total - dot3(
                    nn, hats[:, pivot * 256 : (pivot + 1) * 256], p_high[pivot, child], p_low[pivot, child]
                )
            b_cat[child] = stack(total)
        loads[4].wait()

    def times(value, right):
        value_high, value_low = split(value)
        wide = nt(value_high, right)
        return wide[:, :128] + wide[:, 128:] + nt(value_low, right[:128])

    def tile(index):
        at = (high * 4 + index) % 8
        rows = pl.ds(pl.multiple_of(at * TILE, TILE), TILE)
        total = block_v[rows, :] - times(ubuf[index // 4, index % 4], y_cat[...])
        for child in range(2):
            side, line, found = source(child, 2 + low * 8 + at)
            total = total - times(cbuf[child, side, line], b_cat[child]) * found
        out_ref[0, rows, :] = total

    computing = dict(
        inverse=inverse, pivots=pivots, hat=hat, weight=weight, back=back, narrow=narrow,
        tile=tile,
    )

    held, lines, halves = [], {}, {}

    def release():
        for item in held:
            wires.pair(*item)
        held.clear()

    def pair_kind(name):
        if name[0] == "u":
            return 1 if name[1] == 0 else 3
        return 2 if name[0] == "g" else 0

    for action, name in plan():
        if action == "work":
            release()
            if isinstance(name, tuple):
                computing[name[0]](name[1])
            else:
                computing[name]()
        elif action == "wait":
            release()
            if name == "U":
                loads[2].wait()
                held.append((1, u_slot(0, 0, core)))
            elif name == "G":
                loads[3].wait()
            elif name == "C":
                own_panel()
            elif name == ("cols", "near"):
                pl.when(jnp.logical_or(place == 1, place == 2))(cols_arrive)
            else:
                piece = arrived(name)
                if "xx" in name:
                    halves[name[:-1]] = halves.get(name[:-1], 0) + 1
                    if halves[name[:-1]] == 1:
                        continue
                    step, way = name[1:3] if name[0] == "a" else (0, 1)
                    piece = c_slot(2, -way * step, core, *span(*((0, CUT) if name[0] == "a" else (CUT, TAIL)), step, way))
                wires.arrive(name, piece)
                if name[0] == "a" and LAST in name[1:4]:
                    held.append((0, piece))
                elif name[0] in "ab" and name[1] != "z":
                    line, rows = (name[1:3], (0, CUT)) if name[0] == "a" else ((0, 1), (CUT, TAIL))
                    lines[line, rows] = lines.get((line, rows), 0) + 1
                    if lines[line, rows] == 3:
                        step, way = line
                        held.append((0, c_line(-way * step, core, *span(*rows, step, way))))
                elif name[:2] != ("a", "z"):
                    held.append((pair_kind(name), piece))
        elif name == ("cols", "near"):
            @pl.when(place < 2)
            def _():
                for to_core in range(2):
                    cols_near(to_core).start()
        else:
            wires.send(name, *leaving(name))

    wires.drain()

    @pl.when(place < 2)
    def _():
        for to_core in range(2):
            cols_near(to_core).wait_send()


def local(panel, pattern, child_inverse, ext_map, upper_rows, parent_inverse, update_block):
    anywhere = pl.BlockSpec(memory_space=pltpu.HBM)
    return pl.pallas_call(
        kernel,
        out_shape=pltpu.VMEM((1, 2048, 128), F32),
        in_specs=[anywhere] * 7,
        out_specs=pl.BlockSpec(memory_space=pltpu.VMEM),
        scratch_shapes=[
            pltpu.VMEM((2, 2, 4, TILE, 512), F32),
            pltpu.VMEM((2, 4, TILE, 512), F32),
            pltpu.VMEM((128, 512), F32),
            pltpu.VMEM((2, 128, 512), F32),
            pltpu.VMEM((128, 512), F32),
            pltpu.VMEM((128, 512), F32),
            pltpu.VMEM((512, 512), F32),
            pltpu.VMEM((ROWS, 512), F32),
            pltpu.VMEM((512, 512), F32),
            pltpu.VMEM((2048, 128), F32),
            pltpu.VMEM((2, 2, TILE, 512), BF16),
            pltpu.VMEM((2, 2, TILE, 512), BF16),
            pltpu.VMEM((512, 512), BF16),
            pltpu.VMEM((512, 512), BF16),
            pltpu.VMEM((2, 256, 512), BF16),
            pltpu.VMEM((256, 512), BF16),
            pltpu.SMEM((8, 8), jnp.int32),
            pltpu.SMEM((1, 2, 8), jnp.int32),
            pltpu.SemaphoreType.DMA((7,)),
            pltpu.SemaphoreType.DMA((2,)),
            pltpu.SemaphoreType.DMA((len(messages()[0]) - 11,)),
            pltpu.SemaphoreType.DMA((4,)),
            pltpu.SemaphoreType.DMA((2, 2)),
        ],
        compiler_params=pltpu.CompilerParams(
            collective_id=0, has_side_effects=True, vmem_limit_bytes=60 * 2**20
        ),
    )(ext_map, jnp.swapaxes(pattern, 1, 2), panel, child_inverse, upper_rows, parent_inverse, update_block)


def solution(mesh):
    in_specs = (
        P("cube", "grid", None),
        P("cube", None, None),
        P("cube", None, None),
        P(),
        P("cube", "grid", None),
        P("cube", None, None),
        P("cube", None, "grid"),
    )
    out_specs = P("cube", None, "grid")
    return jax.shard_map(local, mesh=mesh, in_specs=in_specs, out_specs=out_specs, check_vma=False)
```
